512 devices in a mesh: grow: 64 (over x, z_lo, y), lat: 8 (over z_hi, core).
Axes of the slice: x: 4, y: 8, z: 8 (z_hi: 4, z_lo: 2; z = z_hi * 2 + z_lo), core: 2. Of those that a mesh axis runs over, the one named last changes fastest.
Arguments:
- labels: int32 [512, 256, 256], P('grow', 'lat'), may hold values from 0 to 3
- seed_blend: float32 [4, 512, 256, 256], P(None, 'grow', 'lat'), may hold values from 0.02 to 0.6
- potential: float32 [2, 512, 256, 256], P(None, 'grow', 'lat'), may hold values from -3 to 3
- inflow_index: int32 [8, 256, 256], P(None, 'lat'), may hold values from 0 to 15
- liquid_table: float32 [16, 2], replicated, may hold values from -1 to 1
Outputs:
- phase_field: float32 [4, 512, 256, 256], P(None, 'grow', 'lat')
- chem_field: float32 [2, 512, 256, 256], P(None, 'grow', 'lat')
The draws below stay inside these ranges and needn't reach their ends.
All inputs are finite; a program needn't handle non-finite values.
Results may differ from the reference program's by a relative error of at most 0.0001.
Values sent between devices are 32-bit elements; how exact they have to be, the bound alone decides.
No kernel may reach another device: no remote copies, remote signals or barrier semaphores. Data moves between devices by JAX's collectives and lax.ppermute only.
A program may use at most 64 MiB of HBM per device.

```python
import math
import jax
import jax.numpy as jnp

CZ = 8
NY = 256
LIQUIDS = 16
GROWTH_PLANES = 512
NX = 256


def with_ends(values, rng, smallest, high):
    spot = [jax.random.randint(jax.random.fold_in(rng, axis), (), 0, length) for axis, length in enumerate(values.shape)]
    widest = values.shape.index(max(values.shape))
    neighbour = spot[:widest] + [(spot[widest] + 1) % values.shape[widest]] + spot[widest + 1:]
    return values.at[tuple(spot)].set(smallest).at[tuple(neighbour)].set(high)


def steps_of(stream_key, extent, split, smallest, top_value):
    gain, own = 1.0, jax.random.fold_in(stream_key, 6)
    for dim, shards_of in split:
        draws = jnp.exp(jax.random.uniform(jax.random.fold_in(own, dim), (shards_of,), jnp.float32, smallest / len(split), top_value / len(split)))
        gain = gain * jnp.repeat(draws, extent[dim] // shards_of).reshape([-1 if axis == dim else 1 for axis in range(len(extent))])
    return gain


def gaussian(stream_key, dims, width, bound, pieces=(), kind=jnp.bfloat16):
    values = width * jax.random.normal(stream_key, dims, jnp.float32)
    if pieces:
        values = values * steps_of(stream_key, dims, pieces, -0.22, 0.18)
    return jnp.clip(values, -bound, bound).astype(kind)


def setup_inputs(seed: int = 0) -> dict:
    arg_keys = jax.random.split(jax.random.key(seed), 6)
    return {
        "labels": with_ends(jax.random.randint(arg_keys[0], (GROWTH_PLANES, NX, NY), 0, 4), jax.random.fold_in(arg_keys[0], 1), 0, 3).astype(jnp.int32),
        "seed_blend": jnp.clip(jnp.exp(math.log(0.6) - 3.4011974 * jax.random.uniform(arg_keys[1], (4, GROWTH_PLANES, NX, NY), jnp.float32) ** steps_of(arg_keys[1], (4, GROWTH_PLANES, NX, NY), ((1, 64), (2, 8)), -0.2, 0.2)), 0.02, 0.6),
        "potential": gaussian(arg_keys[2], (2, GROWTH_PLANES, NX, NY), 0.5, 3.0, ((1, 64), (2, 8)), jnp.float32),
        "inflow_index": with_ends(jax.random.randint(arg_keys[3], (CZ, NX, NY), 0, LIQUIDS), jax.random.fold_in(arg_keys[3], 1), 0, LIQUIDS - 1).astype(jnp.int32),
        "liquid_table": jnp.clip(jax.random.uniform(arg_keys[4], (LIQUIDS, 2), jnp.float32, -1.0, 1.0), -1.0, 1.0),
    }


offset_table = ((0.0, 0.0), (0.6, -0.3), (-0.4, 0.5), (-0.2, -0.6))
latent_heat = (0.0, 0.8, 0.8, 0.8)
relax_rate = 0.1
diffusion = 0.05


def evolve_fields(padded_fields, thermal_profile):
    centre = padded_fields[:, 1:-1, 1:-1]
    laplace = (padded_fields[:, 2:, 1:-1] + padded_fields[:, :-2, 1:-1]) + (padded_fields[:, 1:-1, 2:] + padded_fields[:, 1:-1, :-2])
    laplace = laplace + (jnp.roll(centre, -1, axis=3) + jnp.roll(centre, 1, axis=3)) - 6.0 * centre
    phases = centre[:4]
    chemical = centre[4:]
    offsets = jnp.array(offset_table, jnp.float32)
    latent_release = jnp.array(latent_heat, jnp.float32)[:, None, None, None]
    free_energy_density = jnp.zeros_like(phases)
    for solute in range(2):
        shifted = chemical[solute][None] + offsets[:, solute][:, None, None, None]
        free_energy_density = free_energy_density + shifted * shifted
    free_energy_density = -0.5 * free_energy_density + latent_release * thermal_profile
    driving = laplace[:4] - phases * (1.0 - phases) * (1.0 - 2.0 * phases) - 2.0 * phases * free_energy_density
    driving = driving - jnp.mean(driving, axis=0, keepdims=True)
    new_phases = phases + relax_rate * driving
    growth = new_phases * new_phases - phases * phases
    susceptible = jnp.sum(new_phases * new_phases, axis=0)
    mobile = diffusion * (0.1 + new_phases[0] * new_phases[0])
    new_chemical = []
    for solute in range(2):
        shifted = chemical[solute][None] + offsets[:, solute][:, None, None, None]
        source = jnp.sum(shifted * growth, axis=0)
        new_chemical.append(chemical[solute] + (mobile * laplace[4 + solute] - source) / susceptible)
    return jnp.concatenate([new_phases, jnp.stack(new_chemical)], axis=0)


def initial(labels, seed_blend, potential):
    kinds = jnp.arange(4, dtype=jnp.int32)[:, None, None, None]
    onehot = (labels[None] == kinds).astype(jnp.float32)
    phases = (onehot + seed_blend) / (1.0 + jnp.sum(seed_blend, axis=0))
    return jnp.concatenate([phases, potential], axis=0)


def inflow_fields(inflow_index, liquid_table):
    kinds = jnp.arange(liquid_table.shape[0], dtype=jnp.int32)[:, None, None, None]
    selected = (inflow_index[None] == kinds).astype(jnp.float32)
    chemical = []
    for solute in range(2):
        chemical.append(jnp.sum(selected * liquid_table[:, solute][:, None, None, None], axis=0))
    liquid = jnp.ones_like(chemical[0])
    solid = jnp.zeros_like(chemical[0])
    return jnp.stack([liquid, solid, solid, solid, chemical[0], chemical[1]])


def reference(labels, seed_blend, potential, inflow_index, liquid_table):
    field_arrays = initial(labels, seed_blend, potential)
    grid_planes = jnp.arange(GROWTH_PLANES, dtype=jnp.int32).astype(jnp.float32)
    thermal_profile = ((2.0 * (grid_planes + 0.5)) / float(GROWTH_PLANES) - 1.0)[:, None, None]
    for turn in range(2):
        padded_fields = jnp.concatenate([field_arrays[:, :1], field_arrays, field_arrays[:, -1:]], axis=1)
        padded_fields = jnp.concatenate([padded_fields[:, :, -1:], padded_fields, padded_fields[:, :, :1]], axis=2)
        field_arrays = evolve_fields(padded_fields, thermal_profile)
    result = jnp.concatenate([field_arrays[:, CZ:], inflow_fields(inflow_index, liquid_table)], axis=1)
    return result[:4], result[4:]
```

```python
import functools

import jax
import jax.numpy as jnp
from jax import lax
from jax.experimental import pallas as pl
from jax.experimental.pallas import tpu as pltpu
from jax.sharding import PartitionSpec as P

offset_table = ((0.0, 0.0), (0.6, -0.3), (-0.4, 0.5), (-0.2, -0.6))
latent_heat = (0.0, 0.8, 0.8, 0.8)
relax_rate = 0.1
diffusion = 0.05

shift = 2
fields = 5
tile = 8

VMEM = pl.BlockSpec(memory_space=pltpu.VMEM)
SMEM = pl.BlockSpec(memory_space=pltpu.SMEM)
ANY = pl.BlockSpec(memory_space=pl.ANY)


def step_tile(below, above, centre, before, after, temp):
    row = lax.broadcasted_iota(jnp.int32, centre[0].shape, 0)
    last = centre[0].shape[0] - 1
    width = centre[0].shape[1]
    laps = []
    for f in range(fields):
        c = centre[f]
        x_minus = pltpu.roll(jnp.where(row == last, before[f], c), 1, 0)
        x_plus = pltpu.roll(jnp.where(row == 0, after[f], c), last, 0)
        y_minus = pltpu.roll(c, 1, 1)
        y_plus = pltpu.roll(c, width - 1, 1)
        laps.append(
            (above[f] + below[f]) + (x_plus + x_minus) + (y_plus + y_minus) - 6.0 * c
        )
    p = list(centre[:3])
    p.append(1.0 - (p[0] + p[1] + p[2]))
    mu = centre[3:]
    common = 1.0 - (mu[0] * mu[0] + mu[1] * mu[1])
    react = []
    for a in range(4):
        e0, e1 = offset_table[a]
        w = common
        if a:
            w = w - (2.0 * e0) * mu[0] - (2.0 * e1) * mu[1]
            w = w + (2.0 * latent_heat[a] * temp - (e0 * e0 + e1 * e1))
        react.append(p[a] * (w + p[a] * (2.0 * p[a] - 3.0)))
    mean = 0.25 * ((react[0] + react[1]) + (react[2] + react[3]))
    new = [p[a] + relax_rate * (laps[a] + (mean - react[a])) for a in range(3)]
    new.append(1.0 - (new[0] + new[1] + new[2]))
    squares = [n * n for n in new]
    growth = [squares[a] - p[a] * p[a] for a in range(4)]
    sus = (squares[0] + squares[1]) + (squares[2] + squares[3])
    grown = (growth[0] + growth[1]) + (growth[2] + growth[3])
    mobile = diffusion * 0.1 + diffusion * squares[0]
    inverse = 1.0 / sus
    out = new[:3]
    for k in range(2):
        source = mu[k] * grown
        for a in range(1, 4):
            source = source + offset_table[a][k] * growth[a]
        out.append(mu[k] + (mobile * laps[3 + k] - source) * inverse)
    return out


def step_plane(src, at, dst, to, temp, tiles, all_tiles):
    for t in range(tiles):
        def rows(plane, u):
            u = (u + all_tiles) % all_tiles
            return [src[plane, f, u * tile : (u + 1) * tile, :] for f in range(fields)]

        new = step_tile(
            rows(at - 1, t), rows(at + 1, t), rows(at, t), rows(at, t - 1), rows(at, t + 1), temp
        )
        for f in range(fields):
            dst[to, f, t * tile : (t + 1) * tile, :] = new[f]


def start_kernel(labels, seed, potential, state, state_send, first_rows, last_rows):
    planes, height = labels.shape[0], labels.shape[1]
    for z in range(planes):
        total = 1.0 + ((seed[0, z] + seed[1, z]) + (seed[2, z] + seed[3, z]))
        scale = 1.0 / total
        lab = labels[z]
        vals = [(jnp.where(lab == a, 1.0, 0.0) + seed[a, z]) * scale for a in range(3)]
        vals += [potential[0, z], potential[1, z]]
        for f in range(fields):
            state[z, f] = vals[f]
            if z < shift + 2:
                state_send[z, f] = vals[f]
            at = 2 * (z * fields + f)
            first_rows[at : at + 2, :] = vals[f][0:2, :]
            last_rows[at : at + 2, :] = vals[f][height - 2 : height, :]


def gather_planes(dst, places, height):
    for i, (main, z, after, before, w) in enumerate(places):
        for f in range(fields):
            dst[i, f, 0:height, :] = main[z, f]
            at = 2 * (w * fields + f)
            dst[i, f, height : height + 2, :] = after[at : at + 2, :]
            dst[i, f, height + 6 : height + 8, :] = before[at : at + 2, :]


def temp_of(place, z, total):
    plane = (place + z).astype(jnp.float32)
    return 2.0 * (plane + 0.5) / float(total) - 1.0


def own_kernel(total, place, state, after, before, done, carry, padded, half):
    planes, height = state.shape[0], state.shape[2]
    tiles = height // tile
    first = shift - 2
    gather_planes(
        padded, [(state, z, after, before, z) for z in range(first, planes)], height
    )
    base = place[0]

    def one(i, _):
        step_plane(padded, i + 1, half, i, temp_of(base, i + first + 1, total), tiles + 1, tiles + 1)
        return 0

    n = planes - first
    lax.fori_loop(0, n - 2, one, 0)

    def two(i, _):
        step_plane(half, i + 1, done, i, temp_of(base, i + shift, total), tiles, tiles + 1)
        return 0

    lax.fori_loop(0, n - 4, two, 0)
    carry[...] = half[n - 4 : n - 2]


def edge_kernel(total, place, state, after, before, upper, upper_after, upper_before, carry,
                done, carry_out, padded, half):
    planes, height = state.shape[0], state.shape[2]
    tiles = height // tile
    base = place[0]
    top = base == total - planes
    gather_planes(
        padded,
        [(state, planes - 2, after, before, planes - 2), (state, planes - 1, after, before, planes - 1)]
        + [(upper, z, upper_after, upper_before, z) for z in range(2)],
        height,
    )

    @pl.when(top)
    def _():
        padded[2] = padded[1]

    half[0:2] = carry[...]

    def one(i, _):
        step_plane(padded, i + 1, half, i + 2, temp_of(base, i + planes - 1, total), tiles + 1, tiles + 1)
        return 0

    lax.fori_loop(0, 2, one, 0)

    @pl.when(top)
    def _():
        half[3] = half[2]

    def two(i, _):
        step_plane(half, i + 1, done, i, temp_of(base, i + planes - 2, total), tiles, tiles + 1)
        return 0

    lax.fori_loop(0, 2, two, 0)
    carry_out[...] = half[2:4]


def upper_kernel(total, place, upper, upper_after, upper_before, carry, done, padded, half):
    height = upper.shape[2]
    tiles = height // tile
    base = place[0]
    planes = place[1]
    gather_planes(padded, [(upper, z, upper_after, upper_before, z) for z in range(shift + 2)], height)
    half[0:2] = carry[...]

    def one(i, _):
        step_plane(padded, i + 1, half, i + 2, temp_of(base + planes, i + 1, total), tiles + 1, tiles + 1)
        return 0

    lax.fori_loop(0, shift, one, 0)

    def two(i, _):
        step_plane(half, i + 1, done, i, temp_of(base + planes, i, total), tiles, tiles + 1)
        return 0

    lax.fori_loop(0, shift, two, 0)


def finish_kernel(total, liquids, place, table, low, middle, high, inflow, phase, chem, extra, sems):
    planes = phase.shape[1]
    parts = [(low, 0, shift), (middle, shift, planes - 2), (high, planes - 2, planes)]
    top = place[0] == total - planes

    @pl.when(jnp.logical_not(top))
    def _():
        copies = []
        for part, first, end in parts:
            for f in range(fields):
                if f < 3:
                    dst = phase.at[f, pl.ds(first, end - first)]
                else:
                    dst = chem.at[f - 3, pl.ds(first, end - first)]
                copy = pltpu.make_async_copy(part.at[:, f], dst, sems.at[len(copies)])
                copy.start()
                copies.append(copy)
        for part, first, end in parts:
            for z in range(first, end):
                extra[0, z] = 1.0 - (part[z - first, 0] + part[z - first, 1] + part[z - first, 2])
        copy = pltpu.make_async_copy(extra.at[0], phase.at[3], sems.at[len(copies)])
        copy.start()
        copies.append(copy)
        for copy in copies:
            copy.wait()

    @pl.when(top)
    def _():
        extra[0] = jnp.ones(extra.shape[1:], jnp.float32)
        extra[1] = jnp.zeros(extra.shape[1:], jnp.float32)

        def lookup(z, _):
            kind = inflow[z]
            for k in range(2):
                value = jnp.zeros(kind.shape, jnp.float32)
                for j in range(liquids):
                    value = jnp.where(kind == j, table[j, k], value)
                extra[2 + k, z] = value
            return 0

        lax.fori_loop(0, planes, lookup, 0)
        copies = []
        pairs = [(0, phase.at[0]), (1, phase.at[1]), (1, phase.at[2]), (1, phase.at[3]),
                 (2, chem.at[0]), (3, chem.at[1])]
        for i, (j, dst) in enumerate(pairs):
            copy = pltpu.make_async_copy(extra.at[j], dst, sems.at[i])
            copy.start()
            copies.append(copy)
        for copy in copies:
            copy.wait()


def f32(*shape):
    return jax.ShapeDtypeStruct(shape, jnp.float32)


def ring(block, axis, distance):
    count = lax.axis_size(axis)
    return lax.ppermute(block, axis, [(i, (i + distance) % count) for i in range(count)])


def body(labels, seed_blend, potential, inflow_index, liquid_table):
    planes, height, width = labels.shape
    total = planes * lax.axis_size("grow")
    base = lax.axis_index("grow") * planes
    place = jnp.stack([base, jnp.int32(planes)]).astype(jnp.int32)
    padded_rows = height + tile
    params = pltpu.CompilerParams(vmem_limit_bytes=24 * 1024 * 1024)

    def call(kernel, out_shape, in_specs, scratch=(), out_specs=None):
        return pl.pallas_call(
            kernel,
            out_shape=out_shape,
            in_specs=in_specs,
            out_specs=out_specs if out_specs is not None else jax.tree.map(lambda _: VMEM, out_shape),
            scratch_shapes=list(scratch),
            compiler_params=params,
        )

    state, send, first_rows, last_rows = call(
        start_kernel,
        (
            f32(planes, fields, height, width),
            f32(shift + 2, fields, height, width),
            f32(2 * planes * fields, width),
            f32(2 * planes * fields, width),
        ),
        [VMEM] * 3,
    )(labels, seed_blend, potential)

    upper = ring(send, "grow", -1)
    after = ring(first_rows, "lat", -1)
    before = ring(last_rows, "lat", 1)

    middle, carry = call(
        functools.partial(own_kernel, total),
        (f32(planes - 2 - shift, fields, height, width), f32(2, fields, padded_rows, width)),
        [SMEM] + [VMEM] * 3,
        [
            pltpu.VMEM((planes - shift + 2, fields, padded_rows, width), jnp.float32),
            pltpu.VMEM((planes - shift, fields, padded_rows, width), jnp.float32),
        ],
    )(place, state, after, before)
    middle_got = ring(middle, "grow", -1)

    rows = (shift + 2) * fields * 2
    upper_first = upper[:, :, 0:2].reshape(rows, width)
    upper_last = upper[:, :, height - 2 : height].reshape(rows, width)
    upper_after = ring(upper_first, "lat", -1)
    upper_before = ring(upper_last, "lat", 1)

    high, carry = call(
        functools.partial(edge_kernel, total),
        (f32(2, fields, height, width), f32(2, fields, padded_rows, width)),
        [SMEM] + [VMEM] * 7,
        [
            pltpu.VMEM((4, fields, padded_rows, width), jnp.float32),
            pltpu.VMEM((4, fields, padded_rows, width), jnp.float32),
        ],
    )(place, state, after, before, upper, upper_after, upper_before, carry)
    high_got = ring(high, "grow", -1)

    low = call(
        functools.partial(upper_kernel, total),
        f32(shift, fields, height, width),
        [SMEM] + [VMEM] * 4,
        [
            pltpu.VMEM((shift + 2, fields, padded_rows, width), jnp.float32),
            pltpu.VMEM((shift + 2, fields, padded_rows, width), jnp.float32),
        ],
    )(place, upper, upper_after, upper_before, carry)

    return call(
        functools.partial(finish_kernel, total, liquid_table.shape[0]),
        (f32(4, planes, height, width), f32(2, planes, height, width)),
        [SMEM, SMEM] + [VMEM] * 4,
        [pltpu.VMEM((4, planes, height, width), jnp.float32), pltpu.SemaphoreType.DMA((3 * fields + 1,))],
        (ANY, ANY),
    )(place, liquid_table, low, middle_got, high_got, inflow_index)


def solution(mesh):
    in_specs = (
        P("grow", "lat", None),
        P(None, "grow", "lat", None),
        P(None, "grow", "lat", None),
        P(None, "lat", None),
        P(),
    )
    out_specs = (P(None, "grow", "lat", None), P(None, "grow", "lat", None))
    return jax.shard_map(body, mesh=mesh, in_specs=in_specs, out_specs=out_specs, check_vma=False)
```

```python
import functools

import jax
import jax.numpy as jnp
from jax import lax
from jax.experimental import pallas as pl
from jax.experimental.pallas import tpu as pltpu
from jax.sharding import PartitionSpec as P

offset_table = ((0.0, 0.0), (0.6, -0.3), (-0.4, 0.5), (-0.2, -0.6))
latent_heat = (0.0, 0.8, 0.8, 0.8)
relax_rate = 0.1
diffusion = 0.05

shift = 3
early = 2
fields = 5
tile = 8
edge_size = -(-2 * fields * (shift + 2) // tile) * tile

VMEM = pl.BlockSpec(memory_space=pltpu.VMEM)
SMEM = pl.BlockSpec(memory_space=pltpu.SMEM)
ANY = pl.BlockSpec(memory_space=pl.ANY)


def step_tile(below, above, centre, before, after, temp):
    row = lax.broadcasted_iota(jnp.int32, centre[0].shape, 0)
    last = centre[0].shape[0] - 1
    width = centre[0].shape[1]
    laps = []
    for f in range(fields):
        c = centre[f]
        x_minus = pltpu.roll(jnp.where(row == last, before[f], c), 1, 0)
        x_plus = pltpu.roll(jnp.where(row == 0, after[f], c), last, 0)
        y_minus = pltpu.roll(c, 1, 1)
        y_plus = pltpu.roll(c, width - 1, 1)
        laps.append(
            (above[f] + below[f]) + (x_plus + x_minus) + (y_plus + y_minus) - 6.0 * c
        )
    p = list(centre[:3])
    p.append(1.0 - (p[0] + p[1] + p[2]))
    mu = centre[3:]
    common = 1.0 - (mu[0] * mu[0] + mu[1] * mu[1])
    react = []
    for a in range(4):
        e0, e1 = offset_table[a]
        w = common
        if a:
            w = w - (2.0 * e0) * mu[0] - (2.0 * e1) * mu[1]
            w = w + (2.0 * latent_heat[a] * temp - (e0 * e0 + e1 * e1))
        react.append(p[a] * (w + p[a] * (2.0 * p[a] - 3.0)))
    mean = 0.25 * ((react[0] + react[1]) + (react[2] + react[3]))
    new = [p[a] + relax_rate * (laps[a] + (mean - react[a])) for a in range(3)]
    new.append(1.0 - (new[0] + new[1] + new[2]))
    squares = [n * n for n in new]
    growth = [squares[a] - p[a] * p[a] for a in range(4)]
    sus = (squares[0] + squares[1]) + (squares[2] + squares[3])
    grown = (growth[0] + growth[1]) + (growth[2] + growth[3])
    mobile = diffusion * 0.1 + diffusion * squares[0]
    inverse = 1.0 / sus
    out = new[:3]
    for k in range(2):
        source = mu[k] * grown
        for a in range(1, 4):
            source = source + offset_table[a][k] * growth[a]
        out.append(mu[k] + (mobile * laps[3 + k] - source) * inverse)
    return out


def step_plane(src, at, dst, to, temp, tiles, all_tiles):
    for t in range(tiles):
        def rows(plane, u):
            u = (u + all_tiles) % all_tiles
            return [src[plane, f, u * tile : (u + 1) * tile, :] for f in range(fields)]

        new = step_tile(
            rows(at - 1, t), rows(at + 1, t), rows(at, t), rows(at, t - 1), rows(at, t + 1), temp
        )
        for f in range(fields):
            dst[to, f, t * tile : (t + 1) * tile, :] = new[f]


def temp_of(z, planes):
    plane = (lax.axis_index("grow") * planes + z).astype(jnp.float32)
    return 2.0 * (plane + 0.5) / float(lax.axis_size("grow") * planes) - 1.0


def is_even():
    return lax.rem(lax.axis_index("lat"), 2) == 0


def is_top():
    return lax.axis_index("grow") == lax.axis_size("grow") - 1


def load_planes(labels, seed, potential, lab, blend, mu, sems, first, count, at):
    zs, to = (pl.ds(first, count), pl.ds(at, count))
    copies = [
        pltpu.make_async_copy(seed.at[:, zs], blend.at[:, to], sems.at[0]),
        pltpu.make_async_copy(labels.at[zs], lab.at[to], sems.at[1]),
        pltpu.make_async_copy(potential.at[:, zs], mu.at[:, to], sems.at[2]),
    ]
    for copy in copies:
        copy.start()
    return copies


def initial_plane(kind, blend, mu, z):
    total = 1.0 + ((blend[0, z] + blend[1, z]) + (blend[2, z] + blend[3, z]))
    scale = 1.0 / total
    vals = [(jnp.where(kind[z] == a, 1.0, 0.0) + blend[a, z]) * scale for a in range(3)]
    return vals + [mu[0, z], mu[1, z]]


def first_kernel(labels, seed, potential, near, token, lab, blend, mu, sems):
    token[...] = jnp.zeros_like(token)
    for copy in load_planes(labels, seed, potential, lab, blend, mu, sems, 0, early, 0):
        copy.wait()
    for z in range(early):
        for f, value in enumerate(initial_plane(lab, blend, mu, z)):
            near[z, f] = value


def start_kernel(labels, seed, potential, token, state, far, inner, outer):
    planes, height = labels.shape[0], labels.shape[1]
    for z in range(planes):
        vals = initial_plane(labels, seed, potential, z)
        for f in range(fields):
            state[z, f] = vals[f]
            if early <= z < shift + 2:
                at = ((z - early) * fields + f) * height
                far[at : at + height, :] = vals[f]

    def edges(after, before):
        for z in range(planes):
            for f in range(fields):
                at = 2 * (z * fields + f)
                before[at : at + 2, :] = state[z, f, 0:2, :]
                after[at : at + 2, :] = state[z, f, height - 2 : height, :]

    @pl.when(is_even())
    def _():
        edges(inner, outer)

    @pl.when(jnp.logical_not(is_even()))
    def _():
        edges(outer, inner)


def pack_kernel(far, inner, outer, near, done, sems):
    at = far.shape[0] - 2 * edge_size
    slot = jnp.where(is_even(), 0, inner.shape[0])
    copies = [
        pltpu.make_async_copy(inner.at[0:edge_size], done.at[at : at + edge_size], sems.at[0]),
        pltpu.make_async_copy(
            outer.at[pl.ds(pl.multiple_of(slot, tile), edge_size)], done.at[at + edge_size :], sems.at[1]
        ),
    ]
    for copy in copies:
        copy.start()
    for copy in copies:
        copy.wait()


def gather_planes(dst, places, height):
    for i, (main, z, _, _) in enumerate(places):
        if len(main.shape) == 4:
            dst[i, :, 0:height, :] = main[z]
        else:
            for f in range(fields):
                dst[i, f, 0:height, :] = main[(z + f) * height : (z + f + 1) * height, :]

    def halo(inner_row, outer_row, slot):
        for i, (_, _, rows, (at_inner, at_outer)) in enumerate(places):
            at_outer = at_outer[slot]
            for f in range(fields):
                for row, at, ref in ((inner_row, at_inner, rows[0]), (outer_row, at_outer, rows[1])):
                    dst[i, f, height + row : height + row + 2, :] = ref[at + 2 * f : at + 2 * f + 2, :]

    @pl.when(is_even())
    def _():
        halo(0, 6, 0)

    @pl.when(jnp.logical_not(is_even()))
    def _():
        halo(6, 0, 1)


def own_places(state, inner, outer, zs):
    width = 2 * fields
    slots = (0, inner.shape[0])
    return [(state, z, (inner, outer), (width * z, [at + width * z for at in slots])) for z in zs]


def upper_places(near, late, zs):
    height = near.shape[2]
    width = 2 * fields
    inner = (shift + 2 - early) * fields * height
    outer = inner + edge_size
    return [
        (near if z < early else late, z if z < early else (z - early) * fields, (late, late),
         (inner + width * z, [outer + width * z] * 2))
        for z in zs
    ]


def steps(padded, half, done, planes, first, known, count, all_tiles):
    def one(i, _):
        step_plane(padded, i + 1, half, i + known, temp_of(i + first - 1 + known, planes), all_tiles, all_tiles)
        return 0

    def two(i, _):
        step_plane(half, i + 1, done, i, temp_of(i + first, planes), all_tiles - 1, all_tiles)
        return 0

    return (
        lambda: lax.fori_loop(0, count + 2 - known, one, 0),
        lambda: lax.fori_loop(0, count, two, 0),
    )


def own_kernel(state, inner, outer, done, carry, padded, half):
    planes, height = state.shape[0], state.shape[2]
    gather_planes(padded, own_places(state, inner, outer, range(shift - 2, planes)), height)
    count = planes - 2 - shift
    one, two = steps(padded, half, done, planes, shift, 0, count, height // tile + 1)
    one()
    two()
    carry[...] = half[count : count + 2]


def edge_kernel(state, inner, outer, near, late, carry, done, carry_out, padded, half):
    planes, height = state.shape[0], state.shape[2]
    gather_planes(
        padded,
        own_places(state, inner, outer, range(planes - 2, planes)) + upper_places(near, late, range(2)),
        height,
    )
    one, two = steps(padded, half, done, planes, planes - 2, 2, 2, height // tile + 1)
    half[0:2] = carry[...]

    @pl.when(is_top())
    def _():
        padded[2] = padded[1]

    one()

    @pl.when(is_top())
    def _():
        half[3] = half[2]

    two()
    carry_out[...] = half[2:4]


def write_planes(parts, phase, chem, extra, sems):
    copies = []
    for part, first in parts:
        count = part.shape[0]
        for f in range(fields):
            to = pl.ds(first, count)
            dst = phase.at[f, to] if f < 3 else chem.at[f - 3, to]
            copies.append(pltpu.make_async_copy(part.at[:, f], dst, sems.at[len(copies)]))
            copies[-1].start()
    for part, first in parts:
        for z in range(part.shape[0]):
            extra[first - parts[0][1] + z] = 1.0 - (part[z, 0] + part[z, 1] + part[z, 2])
    count = sum(part.shape[0] for part, _ in parts)
    copies.append(
        pltpu.make_async_copy(extra.at[0:count], phase.at[3, pl.ds(parts[0][1], count)], sems.at[len(copies)])
    )
    copies[-1].start()
    for copy in copies:
        copy.wait()


def write_liquid(inflow, table, phase, chem, liquid, first, count, sems):
    shape = (count,) + liquid.shape[2:]
    liquid[0, 0:count] = jnp.ones(shape, jnp.float32)
    liquid[1, 0:count] = jnp.zeros(shape, jnp.float32)

    def lookup(z, _):
        kind = inflow[first + z]
        for k in range(2):
            value = jnp.zeros(kind.shape, jnp.float32)
            for j in range(table.shape[0]):
                value = jnp.where(kind == j, table[j, k], value)
            liquid[2 + k, z] = value
        return 0

    lax.fori_loop(0, count, lookup, 0)
    to = pl.ds(first, count)
    pairs = [(0, phase.at[0, to])] + [(1, phase.at[a, to]) for a in range(1, 4)]
    pairs += [(2 + k, chem.at[k, to]) for k in range(2)]
    copies = [pltpu.make_async_copy(liquid.at[j, 0:count], dst, sems.at[i]) for i, (j, dst) in enumerate(pairs)]
    for copy in copies:
        copy.start()
    for copy in copies:
        copy.wait()


def upper_kernel(table, near, late, carry, middle, inflow, phase, chem, padded, half, low, liquid, sems):
    planes, height = phase.shape[1], near.shape[2]

    @pl.when(jnp.logical_not(is_top()))
    def _():
        gather_planes(padded, upper_places(near, late, range(shift + 2)), height)
        half[0:2] = carry[...]
        one, two = steps(padded, half, low, planes, planes, 2, shift, height // tile + 1)
        one()
        two()
        write_planes([(low, 0), (middle, shift)], phase, chem, liquid.at[0], sems)

    @pl.when(is_top())
    def _():
        write_liquid(inflow, table, phase, chem, liquid, 0, planes - 2, sems)


def last_kernel(table, high, inflow, phase_in, chem_in, phase, chem, liquid, sems):
    planes = phase.shape[1]

    @pl.when(jnp.logical_not(is_top()))
    def _():
        write_planes([(high, planes - 2)], phase, chem, liquid.at[0], sems)

    @pl.when(is_top())
    def _():
        write_liquid(inflow, table, phase, chem, liquid, planes - 2, 2, sems)


def f32(*shape):
    return jax.ShapeDtypeStruct(shape, jnp.float32)


def down(block):
    return lax.ppermute(block, "grow", [(i, i - 1) for i in range(1, lax.axis_size("grow"))])


def call(kernel, out_shape, in_specs, scratch=(), out_specs=None, aliases={}, grant=10):
    return pl.pallas_call(
        kernel,
        out_shape=out_shape,
        in_specs=in_specs,
        out_specs=out_specs if out_specs is not None else jax.tree.map(lambda _: VMEM, out_shape),
        scratch_shapes=list(scratch),
        input_output_aliases=aliases,
        compiler_params=pltpu.CompilerParams(vmem_limit_bytes=grant * 1024 * 1024),
    )


def body(labels, seed_blend, potential, inflow_index, liquid_table):
    planes, height, width = labels.shape
    count = lax.axis_size("lat")
    padded_rows = height + tile

    def room(*shape):
        return pltpu.VMEM(shape, jnp.float32)

    near, token = call(
        first_kernel,
        (f32(early, fields, height, width), f32(tile, 128)),
        [ANY] * 3,
        [
            pltpu.VMEM((early, height, width), jnp.int32),
            room(4, early, height, width),
            room(2, early, height, width),
            pltpu.SemaphoreType.DMA((3,)),
        ],
        grant=56,
    )(labels, seed_blend, potential)
    near = down(near)

    edge_rows = 2 * planes * fields
    state, far, inner, outer = call(
        start_kernel,
        (
            f32(planes, fields, height, width),
            f32((shift + 2 - early) * fields * height + 2 * edge_size, width),
            f32(edge_rows, width),
            f32(edge_rows, width),
        ),
        [VMEM] * 3 + [ANY],
    )(labels, seed_blend, potential, token)

    inner = lax.ppermute(inner, "lat", [(i, i ^ 1) for i in range(count)])
    pairs = [[i, (i + 1) % count] for i in range(1, count, 2)]
    outer = lax.all_gather(outer, "lat", axis_index_groups=pairs, tiled=True)
    late = call(
        pack_kernel,
        jax.ShapeDtypeStruct(far.shape, far.dtype),
        [ANY] * 4,
        [pltpu.SemaphoreType.DMA((2,))],
        ANY,
        aliases={0: 0},
    )(far, inner, outer, near)
    late = down(late)

    middle, carry = call(
        own_kernel,
        (f32(planes - 2 - shift, fields, height, width), f32(2, fields, padded_rows, width)),
        [VMEM] * 3,
        [room(planes - shift + 2, fields, padded_rows, width), room(planes - shift, fields, padded_rows, width)],
    )(state, inner, outer)
    middle = down(middle)

    high, carry = call(
        edge_kernel,
        (f32(2, fields, height, width), f32(2, fields, padded_rows, width)),
        [VMEM] * 6,
        [room(4, fields, padded_rows, width), room(4, fields, padded_rows, width)],
    )(state, inner, outer, near, late, carry)
    high = down(high)

    outs = (f32(4, planes, height, width), f32(2, planes, height, width))
    phase, chem = call(
        upper_kernel,
        outs,
        [SMEM] + [VMEM] * 5,
        [
            room(shift + 2, fields, padded_rows, width),
            room(shift + 2, fields, padded_rows, width),
            room(shift, fields, height, width),
            room(4, planes - 2, height, width),
            pltpu.SemaphoreType.DMA((2 * fields + 1,)),
        ],
        (ANY, ANY),
    )(liquid_table, near, late, carry, middle, inflow_index)
    return call(
        last_kernel,
        outs,
        [SMEM] + [VMEM] * 2 + [ANY] * 2,
        [room(4, 2, height, width), pltpu.SemaphoreType.DMA((fields + 1,))],
        (ANY, ANY),
        aliases={3: 0, 4: 1},
    )(liquid_table, high, inflow_index, phase, chem)


def solution(mesh):
    in_specs = (
        P("grow", "lat", None),
        P(None, "grow", "lat", None),
        P(None, "grow", "lat", None),
        P(None, "lat", None),
        P(),
    )
    out_specs = (P(None, "grow", "lat", None), P(None, "grow", "lat", None))
    return jax.shard_map(body, mesh=mesh, in_specs=in_specs, out_specs=out_specs, check_vma=False)
```

```python
import functools

import jax
import jax.numpy as jnp
from jax import lax
from jax.experimental import pallas as pl
from jax.experimental.pallas import tpu as pltpu
from jax.sharding import PartitionSpec as P

offset_table = ((0.0, 0.0), (0.6, -0.3), (-0.4, 0.5), (-0.2, -0.6))
latent_heat = (0.0, 0.8, 0.8, 0.8)
relax_rate = 0.1
diffusion = 0.05

shift = 2
early = 1
fields = 5
tile = 8
edge_size = -(-2 * fields * (shift + 2) // tile) * tile

VMEM = pl.BlockSpec(memory_space=pltpu.VMEM)
SMEM = pl.BlockSpec(memory_space=pltpu.SMEM)
ANY = pl.BlockSpec(memory_space=pl.ANY)


def step_tile(below, above, centre, before, after, temp):
    row = lax.broadcasted_iota(jnp.int32, centre[0].shape, 0)
    last = centre[0].shape[0] - 1
    width = centre[0].shape[1]
    laps = []
    for f in range(fields):
        c = centre[f]
        x_minus = pltpu.roll(jnp.where(row == last, before[f], c), 1, 0)
        x_plus = pltpu.roll(jnp.where(row == 0, after[f], c), last, 0)
        y_minus = pltpu.roll(c, 1, 1)
        y_plus = pltpu.roll(c, width - 1, 1)
        laps.append(
            (above[f] + below[f]) + (x_plus + x_minus) + (y_plus + y_minus) - 6.0 * c
        )
    p = list(centre[:3])
    p.append(1.0 - (p[0] + p[1] + p[2]))
    mu = centre[3:]
    common = 1.0 - (mu[0] * mu[0] + mu[1] * mu[1])
    react = []
    for a in range(4):
        e0, e1 = offset_table[a]
        w = common
        if a:
            w = w - (2.0 * e0) * mu[0] - (2.0 * e1) * mu[1]
            w = w + (2.0 * latent_heat[a] * temp - (e0 * e0 + e1 * e1))
        react.append(p[a] * (w + p[a] * (2.0 * p[a] - 3.0)))
    mean = 0.25 * ((react[0] + react[1]) + (react[2] + react[3]))
    new = [p[a] + relax_rate * (laps[a] + (mean - react[a])) for a in range(3)]
    new.append(1.0 - (new[0] + new[1] + new[2]))
    squares = [n * n for n in new]
    growth = [squares[a] - p[a] * p[a] for a in range(4)]
    sus = (squares[0] + squares[1]) + (squares[2] + squares[3])
    grown = (growth[0] + growth[1]) + (growth[2] + growth[3])
    mobile = diffusion * 0.1 + diffusion * squares[0]
    inverse = 1.0 / sus
    out = new[:3]
    for k in range(2):
        source = mu[k] * grown
        for a in range(1, 4):
            source = source + offset_table[a][k] * growth[a]
        out.append(mu[k] + (mobile * laps[3 + k] - source) * inverse)
    return out


def step_plane(src, at, dst, to, temp, tiles, all_tiles):
    for t in range(tiles):
        def rows(plane, u):
            u = (u + all_tiles) % all_tiles
            return [src[plane, f, u * tile : (u + 1) * tile, :] for f in range(fields)]

        new = step_tile(
            rows(at - 1, t), rows(at + 1, t), rows(at, t), rows(at, t - 1), rows(at, t + 1), temp
        )
        for f in range(fields):
            dst[to, f, t * tile : (t + 1) * tile, :] = new[f]


def temp_of(z, planes):
    plane = (lax.axis_index("grow") * planes + z).astype(jnp.float32)
    return 2.0 * (plane + 0.5) / float(lax.axis_size("grow") * planes) - 1.0


def is_even():
    return lax.rem(lax.axis_index("lat"), 2) == 0


def is_top():
    return lax.axis_index("grow") == lax.axis_size("grow") - 1


def load_planes(labels, seed, potential, lab, blend, mu, sems, first, count, at):
    zs, to = (pl.ds(first, count), pl.ds(at, count))
    copies = [
        pltpu.make_async_copy(seed.at[:, zs], blend.at[:, to], sems.at[0]),
        pltpu.make_async_copy(labels.at[zs], lab.at[to], sems.at[1]),
        pltpu.make_async_copy(potential.at[:, zs], mu.at[:, to], sems.at[2]),
    ]
    for copy in copies:
        copy.start()
    return copies


def initial_plane(kind, blend, mu, z):
    total = 1.0 + ((blend[0, z] + blend[1, z]) + (blend[2, z] + blend[3, z]))
    scale = 1.0 / total
    vals = [(jnp.where(kind[z] == a, 1.0, 0.0) + blend[a, z]) * scale for a in range(3)]
    return vals + [mu[0, z], mu[1, z]]


def first_kernel(labels, seed, potential, near, lab, blend, mu, sems):
    for copy in load_planes(labels, seed, potential, lab, blend, mu, sems, 0, early, 0):
        copy.wait()
    for z in range(early):
        for f, value in enumerate(initial_plane(lab, blend, mu, z)):
            near[z, f] = value


def start_kernel(labels, seed, potential, state, far, inner, outer):
    planes, height = labels.shape[0], labels.shape[1]
    for z in range(planes):
        vals = initial_plane(labels, seed, potential, z)
        for f in range(fields):
            state[z, f] = vals[f]
            if early <= z < shift + 2:
                at = ((z - early) * fields + f) * height
                far[at : at + height, :] = vals[f]

    def edges(after, before):
        for z in range(planes):
            for f in range(fields):
                at = 2 * (z * fields + f)
                before[at : at + 2, :] = state[z, f, 0:2, :]
                after[at : at + 2, :] = state[z, f, height - 2 : height, :]

    @pl.when(is_even())
    def _():
        edges(inner, outer)

    @pl.when(jnp.logical_not(is_even()))
    def _():
        edges(outer, inner)


def pack_kernel(far, inner, outer, near, done, sems):
    at = far.shape[0] - 2 * edge_size
    slot = jnp.where(is_even(), 0, inner.shape[0])
    copies = [
        pltpu.make_async_copy(inner.at[0:edge_size], done.at[at : at + edge_size], sems.at[0]),
        pltpu.make_async_copy(
            outer.at[pl.ds(pl.multiple_of(slot, tile), edge_size)], done.at[at + edge_size :], sems.at[1]
        ),
    ]
    for copy in copies:
        copy.start()
    for copy in copies:
        copy.wait()


def gather_planes(dst, places, height):
    for i, (main, z, _, _) in enumerate(places):
        if len(main.shape) == 4:
            dst[i, :, 0:height, :] = main[z]
        else:
            for f in range(fields):
                dst[i, f, 0:height, :] = main[(z + f) * height : (z + f + 1) * height, :]

    def halo(inner_row, outer_row, slot):
        for i, (_, _, rows, (at_inner, at_outer)) in enumerate(places):
            at_outer = at_outer[slot]
            for f in range(fields):
                for row, at, ref in ((inner_row, at_inner, rows[0]), (outer_row, at_outer, rows[1])):
                    dst[i, f, height + row : height + row + 2, :] = ref[at + 2 * f : at + 2 * f + 2, :]

    @pl.when(is_even())
    def _():
        halo(0, 6, 0)

    @pl.when(jnp.logical_not(is_even()))
    def _():
        halo(6, 0, 1)


def own_places(state, inner, outer, zs):
    width = 2 * fields
    slots = (0, inner.shape[0])
    return [(state, z, (inner, outer), (width * z, [at + width * z for at in slots])) for z in zs]


def upper_places(near, late, zs):
    height = near.shape[2]
    width = 2 * fields
    inner = (shift + 2 - early) * fields * height
    outer = inner + edge_size
    return [
        (near if z < early else late, z if z < early else (z - early) * fields, (late, late),
         (inner + width * z, [outer + width * z] * 2))
        for z in zs
    ]


def steps(padded, half, done, planes, first, known, count, all_tiles):
    def one(i, _):
        step_plane(padded, i + 1, half, i + known, temp_of(i + first - 1 + known, planes), all_tiles, all_tiles)
        return 0

    def two(i, _):
        step_plane(half, i + 1, done, i, temp_of(i + first, planes), all_tiles - 1, all_tiles)
        return 0

    return (
        lambda: lax.fori_loop(0, count + 2 - known, one, 0),
        lambda: lax.fori_loop(0, count, two, 0),
    )


def own_kernel(state, inner, outer, done, carry, padded, half):
    planes, height = state.shape[0], state.shape[2]
    gather_planes(padded, own_places(state, inner, outer, range(shift - 2, planes)), height)
    count = planes - 2 - shift
    one, two = steps(padded, half, done, planes, shift, 0, count, height // tile + 1)
    one()
    two()
    carry[...] = half[count : count + 2]


def edge_kernel(state, inner, outer, near, late, carry, done, carry_out, padded, half):
    planes, height = state.shape[0], state.shape[2]
    gather_planes(
        padded,
        own_places(state, inner, outer, range(planes - 2, planes)) + upper_places(near, late, range(2)),
        height,
    )
    one, two = steps(padded, half, done, planes, planes - 2, 2, 2, height // tile + 1)
    half[0:2] = carry[...]

    @pl.when(is_top())
    def _():
        padded[2] = padded[1]

    one()

    @pl.when(is_top())
    def _():
        half[3] = half[2]

    two()
    carry_out[...] = half[2:4]


def write_planes(parts, phase, chem, extra, sems):
    copies = []
    for part, first in parts:
        count = part.shape[0]
        for f in range(fields):
            to = pl.ds(first, count)
            dst = phase.at[f, to] if f < 3 else chem.at[f - 3, to]
            copies.append(pltpu.make_async_copy(part.at[:, f], dst, sems.at[len(copies)]))
            copies[-1].start()
    for part, first in parts:
        for z in range(part.shape[0]):
            extra[first - parts[0][1] + z] = 1.0 - (part[z, 0] + part[z, 1] + part[z, 2])
    count = sum(part.shape[0] for part, _ in parts)
    copies.append(
        pltpu.make_async_copy(extra.at[0:count], phase.at[3, pl.ds(parts[0][1], count)], sems.at[len(copies)])
    )
    copies[-1].start()
    for copy in copies:
        copy.wait()


def write_liquid(inflow, table, phase, chem, liquid, first, count, sems):
    shape = (count,) + liquid.shape[2:]
    liquid[0, 0:count] = jnp.ones(shape, jnp.float32)
    liquid[1, 0:count] = jnp.zeros(shape, jnp.float32)

    def lookup(z, _):
        kind = inflow[first + z]
        for k in range(2):
            value = jnp.zeros(kind.shape, jnp.float32)
            for j in range(table.shape[0]):
                value = jnp.where(kind == j, table[j, k], value)
            liquid[2 + k, z] = value
        return 0

    lax.fori_loop(0, count, lookup, 0)
    to = pl.ds(first, count)
    pairs = [(0, phase.at[0, to])] + [(1, phase.at[a, to]) for a in range(1, 4)]
    pairs += [(2 + k, chem.at[k, to]) for k in range(2)]
    copies = [pltpu.make_async_copy(liquid.at[j, 0:count], dst, sems.at[i]) for i, (j, dst) in enumerate(pairs)]
    for copy in copies:
        copy.start()
    for copy in copies:
        copy.wait()


def upper_kernel(table, near, late, carry, middle, inflow, phase, chem, padded, half, low, liquid, sems):
    planes, height = phase.shape[1], near.shape[2]

    @pl.when(jnp.logical_not(is_top()))
    def _():
        gather_planes(padded, upper_places(near, late, range(shift + 2)), height)
        half[0:2] = carry[...]
        one, two = steps(padded, half, low, planes, planes, 2, shift, height // tile + 1)
        one()
        two()
        write_planes([(low, 0), (middle, shift)], phase, chem, liquid.at[0], sems)

    @pl.when(is_top())
    def _():
        write_liquid(inflow, table, phase, chem, liquid, 0, planes - 2, sems)


def last_kernel(table, high, inflow, phase_in, chem_in, phase, chem, liquid, sems):
    planes = phase.shape[1]

    @pl.when(jnp.logical_not(is_top()))
    def _():
        write_planes([(high, planes - 2)], phase, chem, liquid.at[0], sems)

    @pl.when(is_top())
    def _():
        write_liquid(inflow, table, phase, chem, liquid, planes - 2, 2, sems)


def f32(*shape):
    return jax.ShapeDtypeStruct(shape, jnp.float32)


def down(block):
    return lax.ppermute(block, "grow", [(i, i - 1) for i in range(1, lax.axis_size("grow"))])


def call(kernel, out_shape, in_specs, scratch=(), out_specs=None, aliases={}, grant=10):
    return pl.pallas_call(
        kernel,
        out_shape=out_shape,
        in_specs=in_specs,
        out_specs=out_specs if out_specs is not None else jax.tree.map(lambda _: VMEM, out_shape),
        scratch_shapes=list(scratch),
        input_output_aliases=aliases,
        compiler_params=pltpu.CompilerParams(vmem_limit_bytes=grant * 1024 * 1024),
    )


def body(labels, seed_blend, potential, inflow_index, liquid_table):
    planes, height, width = labels.shape
    count = lax.axis_size("lat")
    padded_rows = height + tile

    def room(*shape):
        return pltpu.VMEM(shape, jnp.float32)

    near = call(
        first_kernel,
        f32(early, fields, height, width),
        [ANY] * 3,
        [
            pltpu.VMEM((early, height, width), jnp.int32),
            room(4, early, height, width),
            room(2, early, height, width),
            pltpu.SemaphoreType.DMA((3,)),
        ],
        grant=56,
    )(labels, seed_blend, potential)
    near = down(near)

    edge_rows = 2 * planes * fields
    state, far, inner, outer = call(
        start_kernel,
        (
            f32(planes, fields, height, width),
            f32((shift + 2 - early) * fields * height + 2 * edge_size, width),
            f32(edge_rows, width),
            f32(edge_rows, width),
        ),
        [VMEM] * 3,
    )(labels, seed_blend, potential)

    inner = lax.ppermute(inner, "lat", [(i, i ^ 1) for i in range(count)])
    pairs = [[i, (i + 1) % count] for i in range(1, count, 2)]
    outer = lax.all_gather(outer, "lat", axis_index_groups=pairs, tiled=True)
    late = call(
        pack_kernel,
        jax.ShapeDtypeStruct(far.shape, far.dtype),
        [ANY] * 4,
        [pltpu.SemaphoreType.DMA((2,))],
        ANY,
        aliases={0: 0},
    )(far, inner, outer, near)
    late = down(late)

    middle, carry = call(
        own_kernel,
        (f32(planes - 2 - shift, fields, height, width), f32(2, fields, padded_rows, width)),
        [VMEM] * 3,
        [room(planes - shift + 2, fields, padded_rows, width), room(planes - shift, fields, padded_rows, width)],
    )(state, inner, outer)
    middle = down(middle)

    high, carry = call(
        edge_kernel,
        (f32(2, fields, height, width), f32(2, fields, padded_rows, width)),
        [VMEM] * 6,
        [room(4, fields, padded_rows, width), room(4, fields, padded_rows, width)],
    )(state, inner, outer, near, late, carry)
    high = down(high)

    outs = (f32(4, planes, height, width), f32(2, planes, height, width))
    phase, chem = call(
        upper_kernel,
        outs,
        [SMEM] + [VMEM] * 5,
        [
            room(shift + 2, fields, padded_rows, width),
            room(shift + 2, fields, padded_rows, width),
            room(shift, fields, height, width),
            room(4, planes - 2, height, width),
            pltpu.SemaphoreType.DMA((2 * fields + 1,)),
        ],
        (ANY, ANY),
    )(liquid_table, near, late, carry, middle, inflow_index)
    return call(
        last_kernel,
        outs,
        [SMEM] + [VMEM] * 2 + [ANY] * 2,
        [room(4, 2, height, width), pltpu.SemaphoreType.DMA((fields + 1,))],
        (ANY, ANY),
        aliases={3: 0, 4: 1},
    )(liquid_table, high, inflow_index, phase, chem)


def solution(mesh):
    in_specs = (
        P("grow", "lat", None),
        P(None, "grow", "lat", None),
        P(None, "grow", "lat", None),
        P(None, "lat", None),
        P(),
    )
    out_specs = (P(None, "grow", "lat", None), P(None, "grow", "lat", None))
    return jax.shard_map(body, mesh=mesh, in_specs=in_specs, out_specs=out_specs, check_vma=False)
```

```python
import functools

import jax
import jax.numpy as jnp
from jax import lax
from jax.experimental import pallas as pl
from jax.experimental.pallas import tpu as pltpu
from jax.sharding import PartitionSpec as P

offset_table = ((0.0, 0.0), (0.6, -0.3), (-0.4, 0.5), (-0.2, -0.6))
latent_heat = (0.0, 0.8, 0.8, 0.8)
relax_rate = 0.1
diffusion = 0.05

shift = 2
early = 1
fields = 5
tile = 8
edge_size = -(-2 * fields * (shift + 2) // tile) * tile

VMEM = pl.BlockSpec(memory_space=pltpu.VMEM)
SMEM = pl.BlockSpec(memory_space=pltpu.SMEM)
ANY = pl.BlockSpec(memory_space=pl.ANY)


def step_tile(below, above, centre, before, after, temp):
    row = lax.broadcasted_iota(jnp.int32, centre[0].shape, 0)
    last = centre[0].shape[0] - 1
    width = centre[0].shape[1]
    laps = []
    for f in range(fields):
        c = centre[f]
        x_minus = pltpu.roll(jnp.where(row == last, before[f], c), 1, 0)
        x_plus = pltpu.roll(jnp.where(row == 0, after[f], c), last, 0)
        y_minus = pltpu.roll(c, 1, 1)
        y_plus = pltpu.roll(c, width - 1, 1)
        laps.append(
            (above[f] + below[f]) + (x_plus + x_minus) + (y_plus + y_minus) - 6.0 * c
        )
    p = list(centre[:3])
    p.append(1.0 - (p[0] + p[1] + p[2]))
    mu = centre[3:]
    common = 1.0 - (mu[0] * mu[0] + mu[1] * mu[1])
    react = []
    for a in range(4):
        e0, e1 = offset_table[a]
        w = common
        if a:
            w = w - (2.0 * e0) * mu[0] - (2.0 * e1) * mu[1]
            w = w + (2.0 * latent_heat[a] * temp - (e0 * e0 + e1 * e1))
        react.append(p[a] * (w + p[a] * (2.0 * p[a] - 3.0)))
    mean = 0.25 * ((react[0] + react[1]) + (react[2] + react[3]))
    new = [p[a] + relax_rate * (laps[a] + (mean - react[a])) for a in range(3)]
    new.append(1.0 - (new[0] + new[1] + new[2]))
    squares = [n * n for n in new]
    growth = [squares[a] - p[a] * p[a] for a in range(4)]
    sus = (squares[0] + squares[1]) + (squares[2] + squares[3])
    grown = (growth[0] + growth[1]) + (growth[2] + growth[3])
    mobile = diffusion * 0.1 + diffusion * squares[0]
    inverse = 1.0 / sus
    out = new[:3]
    for k in range(2):
        source = mu[k] * grown
        for a in range(1, 4):
            source = source + offset_table[a][k] * growth[a]
        out.append(mu[k] + (mobile * laps[3 + k] - source) * inverse)
    return out


def step_plane(src, at, dst, to, temp, tiles, all_tiles):
    for t in range(tiles):
        def rows(plane, u):
            u = (u + all_tiles) % all_tiles
            return [src[plane, f, u * tile : (u + 1) * tile, :] for f in range(fields)]

        new = step_tile(
            rows(at - 1, t), rows(at + 1, t), rows(at, t), rows(at, t - 1), rows(at, t + 1), temp
        )
        for f in range(fields):
            dst[to, f, t * tile : (t + 1) * tile, :] = new[f]


def temp_of(z, planes):
    plane = (lax.axis_index("grow") * planes + z).astype(jnp.float32)
    return 2.0 * (plane + 0.5) / float(lax.axis_size("grow") * planes) - 1.0


def is_even():
    return lax.rem(lax.axis_index("lat"), 2) == 0


def is_top():
    return lax.axis_index("grow") == lax.axis_size("grow") - 1


def load_planes(labels, seed, potential, lab, blend, mu, sems, first, count, at):
    zs, to = (pl.ds(first, count), pl.ds(at, count))
    copies = [
        pltpu.make_async_copy(seed.at[:, zs], blend.at[:, to], sems.at[0]),
        pltpu.make_async_copy(labels.at[zs], lab.at[to], sems.at[1]),
        pltpu.make_async_copy(potential.at[:, zs], mu.at[:, to], sems.at[2]),
    ]
    for copy in copies:
        copy.start()
    return copies


def initial_plane(kind, blend, mu, z):
    total = 1.0 + ((blend[0, z] + blend[1, z]) + (blend[2, z] + blend[3, z]))
    scale = 1.0 / total
    vals = [(jnp.where(kind[z] == a, 1.0, 0.0) + blend[a, z]) * scale for a in range(3)]
    return vals + [mu[0, z], mu[1, z]]


def first_kernel(labels, seed, potential, near, lab, blend, mu, sems):
    for copy in load_planes(labels, seed, potential, lab, blend, mu, sems, 0, early, 0):
        copy.wait()
    for z in range(early):
        for f, value in enumerate(initial_plane(lab, blend, mu, z)):
            near[z, f] = value


def start_kernel(labels, seed, potential, state, far, inner, outer):
    planes, height = labels.shape[0], labels.shape[1]
    for z in range(planes):
        vals = initial_plane(labels, seed, potential, z)
        for f in range(fields):
            state[z, f] = vals[f]
            if early <= z < shift + 2:
                at = ((z - early) * fields + f) * height
                far[at : at + height, :] = vals[f]

    def edges(after, before):
        for z in range(planes):
            for f in range(fields):
                at = 2 * (z * fields + f)
                before[at : at + 2, :] = state[z, f, 0:2, :]
                after[at : at + 2, :] = state[z, f, height - 2 : height, :]

    @pl.when(is_even())
    def _():
        edges(inner, outer)

    @pl.when(jnp.logical_not(is_even()))
    def _():
        edges(outer, inner)


def pack_kernel(far, inner, outer, near, done, inner_out, sem):
    at = far.shape[0] - edge_size
    slot = jnp.where(is_even(), 0, inner.shape[0])
    copy = pltpu.make_async_copy(outer.at[pl.ds(pl.multiple_of(slot, tile), edge_size)], done.at[at:], sem)
    copy.start()
    copy.wait()


def rows_kernel(near, late, inner):
    height = near.shape[2]

    def edges(row):
        for z in range(shift + 2):
            for f in range(fields):
                at = 2 * (z * fields + f)
                if z < early:
                    inner[at : at + 2, :] = near[z, f, row : row + 2, :]
                else:
                    first = ((z - early) * fields + f) * height + row
                    inner[at : at + 2, :] = late[first : first + 2, :]

    @pl.when(is_even())
    def _():
        edges(height - 2)

    @pl.when(jnp.logical_not(is_even()))
    def _():
        edges(0)


def gather_planes(dst, places, height):
    for i, (main, z, _, _) in enumerate(places):
        if len(main.shape) == 4:
            dst[i, :, 0:height, :] = main[z]
        else:
            for f in range(fields):
                dst[i, f, 0:height, :] = main[(z + f) * height : (z + f + 1) * height, :]

    def halo(inner_row, outer_row, slot):
        for i, (_, _, rows, (at_inner, at_outer)) in enumerate(places):
            at_outer = at_outer[slot]
            for f in range(fields):
                for row, at, ref in ((inner_row, at_inner, rows[0]), (outer_row, at_outer, rows[1])):
                    dst[i, f, height + row : height + row + 2, :] = ref[at + 2 * f : at + 2 * f + 2, :]

    @pl.when(is_even())
    def _():
        halo(0, 6, 0)

    @pl.when(jnp.logical_not(is_even()))
    def _():
        halo(6, 0, 1)


def own_places(state, inner, outer, zs):
    width = 2 * fields
    slots = (0, inner.shape[0])
    return [(state, z, (inner, outer), (width * z, [at + width * z for at in slots])) for z in zs]


def upper_places(near, late, inner, zs):
    width = 2 * fields
    outer = (shift + 2 - early) * fields * near.shape[2]
    return [
        (near if z < early else late, z if z < early else (z - early) * fields, (inner, late),
         (width * z, [outer + width * z] * 2))
        for z in zs
    ]


def steps(padded, half, done, planes, first, known, count, all_tiles):
    def one(i, _):
        step_plane(padded, i + 1, half, i + known, temp_of(i + first - 1 + known, planes), all_tiles, all_tiles)
        return 0

    def two(i, _):
        step_plane(half, i + 1, done, i, temp_of(i + first, planes), all_tiles - 1, all_tiles)
        return 0

    return (
        lambda: lax.fori_loop(0, count + 2 - known, one, 0),
        lambda: lax.fori_loop(0, count, two, 0),
    )


def own_kernel(state, inner, outer, done, carry, padded, half):
    planes, height = state.shape[0], state.shape[2]
    gather_planes(padded, own_places(state, inner, outer, range(shift - 2, planes)), height)
    count = planes - 2 - shift
    one, two = steps(padded, half, done, planes, shift, 0, count, height // tile + 1)
    one()
    two()
    carry[...] = half[count : count + 2]


def edge_kernel(state, inner, outer, near, late, upper_inner, carry, done, carry_out, padded, half):
    planes, height = state.shape[0], state.shape[2]
    gather_planes(
        padded,
        own_places(state, inner, outer, range(planes - 2, planes)) + upper_places(near, late, upper_inner, range(2)),
        height,
    )
    one, two = steps(padded, half, done, planes, planes - 2, 2, 2, height // tile + 1)
    half[0:2] = carry[...]

    @pl.when(is_top())
    def _():
        padded[2] = padded[1]

    one()

    @pl.when(is_top())
    def _():
        half[3] = half[2]

    two()
    carry_out[...] = half[2:4]


def write_planes(parts, phase, chem, extra, sems):
    copies = []
    for part, first in parts:
        count = part.shape[0]
        for f in range(fields):
            to = pl.ds(first, count)
            dst = phase.at[f, to] if f < 3 else chem.at[f - 3, to]
            copies.append(pltpu.make_async_copy(part.at[:, f], dst, sems.at[len(copies)]))
            copies[-1].start()
    for part, first in parts:
        for z in range(part.shape[0]):
            extra[first - parts[0][1] + z] = 1.0 - (part[z, 0] + part[z, 1] + part[z, 2])
    count = sum(part.shape[0] for part, _ in parts)
    copies.append(
        pltpu.make_async_copy(extra.at[0:count], phase.at[3, pl.ds(parts[0][1], count)], sems.at[len(copies)])
    )
    copies[-1].start()
    for copy in copies:
        copy.wait()


def write_liquid(inflow, table, phase, chem, liquid, first, count, sems):
    shape = (count,) + liquid.shape[2:]
    liquid[0, 0:count] = jnp.ones(shape, jnp.float32)
    liquid[1, 0:count] = jnp.zeros(shape, jnp.float32)

    def lookup(z, _):
        kind = inflow[first + z]
        for k in range(2):
            value = jnp.zeros(kind.shape, jnp.float32)
            for j in range(table.shape[0]):
                value = jnp.where(kind == j, table[j, k], value)
            liquid[2 + k, z] = value
        return 0

    lax.fori_loop(0, count, lookup, 0)
    to = pl.ds(first, count)
    pairs = [(0, phase.at[0, to])] + [(1, phase.at[a, to]) for a in range(1, 4)]
    pairs += [(2 + k, chem.at[k, to]) for k in range(2)]
    copies = [pltpu.make_async_copy(liquid.at[j, 0:count], dst, sems.at[i]) for i, (j, dst) in enumerate(pairs)]
    for copy in copies:
        copy.start()
    for copy in copies:
        copy.wait()


def upper_kernel(table, near, late, upper_inner, carry, middle, inflow, phase, chem, padded, half, low, liquid, sems):
    planes, height = phase.shape[1], near.shape[2]

    @pl.when(jnp.logical_not(is_top()))
    def _():
        gather_planes(padded, upper_places(near, late, upper_inner, range(shift + 2)), height)
        half[0:2] = carry[...]
        one, two = steps(padded, half, low, planes, planes, 2, shift, height // tile + 1)
        one()
        two()
        write_planes([(low, 0), (middle, shift)], phase, chem, liquid.at[0], sems)

    @pl.when(is_top())
    def _():
        write_liquid(inflow, table, phase, chem, liquid, 0, planes - 2, sems)


def last_kernel(table, high, inflow, phase_in, chem_in, phase, chem, liquid, sems):
    planes = phase.shape[1]

    @pl.when(jnp.logical_not(is_top()))
    def _():
        write_planes([(high, planes - 2)], phase, chem, liquid.at[0], sems)

    @pl.when(is_top())
    def _():
        write_liquid(inflow, table, phase, chem, liquid, planes - 2, 2, sems)


def f32(*shape):
    return jax.ShapeDtypeStruct(shape, jnp.float32)


def down(block):
    return lax.ppermute(block, "grow", [(i, i - 1) for i in range(1, lax.axis_size("grow"))])


def call(kernel, out_shape, in_specs, scratch=(), out_specs=None, aliases={}, grant=10):
    return pl.pallas_call(
        kernel,
        out_shape=out_shape,
        in_specs=in_specs,
        out_specs=out_specs if out_specs is not None else jax.tree.map(lambda _: VMEM, out_shape),
        scratch_shapes=list(scratch),
        input_output_aliases=aliases,
        compiler_params=pltpu.CompilerParams(vmem_limit_bytes=grant * 1024 * 1024),
    )


def body(labels, seed_blend, potential, inflow_index, liquid_table):
    planes, height, width = labels.shape
    count = lax.axis_size("lat")
    padded_rows = height + tile

    def room(*shape):
        return pltpu.VMEM(shape, jnp.float32)

    near = call(
        first_kernel,
        f32(early, fields, height, width),
        [ANY] * 3,
        [
            pltpu.VMEM((early, height, width), jnp.int32),
            room(4, early, height, width),
            room(2, early, height, width),
            pltpu.SemaphoreType.DMA((3,)),
        ],
        grant=56,
    )(labels, seed_blend, potential)
    near = down(near)

    edge_rows = 2 * planes * fields
    state, far, inner, outer = call(
        start_kernel,
        (
            f32(planes, fields, height, width),
            f32((shift + 2 - early) * fields * height + edge_size, width),
            f32(edge_rows, width),
            f32(edge_rows, width),
        ),
        [VMEM] * 3,
    )(labels, seed_blend, potential)

    swap = [(i, i ^ 1) for i in range(count)]
    pairs = [[i, (i + 1) % count] for i in range(1, count, 2)]
    outer = lax.all_gather(outer, "lat", axis_index_groups=pairs, tiled=True)
    late, inner = call(
        pack_kernel,
        (jax.ShapeDtypeStruct(far.shape, far.dtype), jax.ShapeDtypeStruct(inner.shape, inner.dtype)),
        [ANY] * 4,
        [pltpu.SemaphoreType.DMA],
        (ANY, ANY),
        aliases={0: 0, 1: 1},
    )(far, inner, outer, near)
    late = down(late)
    inner = lax.ppermute(inner, "lat", swap)

    middle, carry = call(
        own_kernel,
        (f32(planes - 2 - shift, fields, height, width), f32(2, fields, padded_rows, width)),
        [VMEM] * 3,
        [room(planes - shift + 2, fields, padded_rows, width), room(planes - shift, fields, padded_rows, width)],
    )(state, inner, outer)
    middle = down(middle)

    upper_inner = call(rows_kernel, f32(edge_size, width), [VMEM] * 2)(near, late)
    upper_inner = lax.ppermute(upper_inner, "lat", swap)

    high, carry = call(
        edge_kernel,
        (f32(2, fields, height, width), f32(2, fields, padded_rows, width)),
        [VMEM] * 7,
        [room(4, fields, padded_rows, width), room(4, fields, padded_rows, width)],
    )(state, inner, outer, near, late, upper_inner, carry)
    high = down(high)

    outs = (f32(4, planes, height, width), f32(2, planes, height, width))
    phase, chem = call(
        upper_kernel,
        outs,
        [SMEM] + [VMEM] * 6,
        [
            room(shift + 2, fields, padded_rows, width),
            room(shift + 2, fields, padded_rows, width),
            room(shift, fields, height, width),
            room(4, planes - 2, height, width),
            pltpu.SemaphoreType.DMA((2 * fields + 1,)),
        ],
        (ANY, ANY),
    )(liquid_table, near, late, upper_inner, carry, middle, inflow_index)
    return call(
        last_kernel,
        outs,
        [SMEM] + [VMEM] * 2 + [ANY] * 2,
        [room(4, 2, height, width), pltpu.SemaphoreType.DMA((fields + 1,))],
        (ANY, ANY),
        aliases={3: 0, 4: 1},
    )(liquid_table, high, inflow_index, phase, chem)


def solution(mesh):
    in_specs = (
        P("grow", "lat", None),
        P(None, "grow", "lat", None),
        P(None, "grow", "lat", None),
        P(None, "lat", None),
        P(),
    )
    out_specs = (P(None, "grow", "lat", None), P(None, "grow", "lat", None))
    return jax.shard_map(body, mesh=mesh, in_specs=in_specs, out_specs=out_specs, check_vma=False)
```

```python
import functools

import jax
import jax.numpy as jnp
from jax import lax
from jax.experimental import pallas as pl
from jax.experimental.pallas import tpu as pltpu
from jax.sharding import PartitionSpec as P

offset_table = ((0.0, 0.0), (0.6, -0.3), (-0.4, 0.5), (-0.2, -0.6))
latent_heat = (0.0, 0.8, 0.8, 0.8)
relax_rate = 0.1
diffusion = 0.05

shift = 2
early = 1
fields = 5
tile = 8
edge_size = -(-2 * fields * (shift + 2) // tile) * tile

VMEM = pl.BlockSpec(memory_space=pltpu.VMEM)
SMEM = pl.BlockSpec(memory_space=pltpu.SMEM)
ANY = pl.BlockSpec(memory_space=pl.ANY)


def step_tile(below, above, centre, before, after, temp):
    row = lax.broadcasted_iota(jnp.int32, centre[0].shape, 0)
    last = centre[0].shape[0] - 1
    width = centre[0].shape[1]
    laps = []
    for f in range(fields):
        c = centre[f]
        x_minus = pltpu.roll(jnp.where(row == last, before[f], c), 1, 0)
        x_plus = pltpu.roll(jnp.where(row == 0, after[f], c), last, 0)
        y_minus = pltpu.roll(c, 1, 1)
        y_plus = pltpu.roll(c, width - 1, 1)
        laps.append(
            (above[f] + below[f]) + (x_plus + x_minus) + (y_plus + y_minus) - 6.0 * c
        )
    p = list(centre[:3])
    p.append(1.0 - (p[0] + p[1] + p[2]))
    mu = centre[3:]
    common = 1.0 - (mu[0] * mu[0] + mu[1] * mu[1])
    react = []
    for a in range(4):
        e0, e1 = offset_table[a]
        w = common
        if a:
            w = w - (2.0 * e0) * mu[0] - (2.0 * e1) * mu[1]
            w = w + (2.0 * latent_heat[a] * temp - (e0 * e0 + e1 * e1))
        react.append(p[a] * (w + p[a] * (2.0 * p[a] - 3.0)))
    mean = 0.25 * ((react[0] + react[1]) + (react[2] + react[3]))
    new = [p[a] + relax_rate * (laps[a] + (mean - react[a])) for a in range(3)]
    new.append(1.0 - (new[0] + new[1] + new[2]))
    squares = [n * n for n in new]
    growth = [squares[a] - p[a] * p[a] for a in range(4)]
    sus = (squares[0] + squares[1]) + (squares[2] + squares[3])
    grown = (growth[0] + growth[1]) + (growth[2] + growth[3])
    mobile = diffusion * 0.1 + diffusion * squares[0]
    inverse = 1.0 / sus
    out = new[:3]
    for k in range(2):
        source = mu[k] * grown
        for a in range(1, 4):
            source = source + offset_table[a][k] * growth[a]
        out.append(mu[k] + (mobile * laps[3 + k] - source) * inverse)
    return out


def step_plane(src, at, dst, to, temp, tiles, all_tiles):
    for t in range(tiles):
        def rows(plane, u):
            u = (u + all_tiles) % all_tiles
            return [src[plane, f, u * tile : (u + 1) * tile, :] for f in range(fields)]

        new = step_tile(
            rows(at - 1, t), rows(at + 1, t), rows(at, t), rows(at, t - 1), rows(at, t + 1), temp
        )
        for f in range(fields):
            dst[to, f, t * tile : (t + 1) * tile, :] = new[f]


def temp_of(z, planes):
    plane = (lax.axis_index("grow") * planes + z).astype(jnp.float32)
    return 2.0 * (plane + 0.5) / float(lax.axis_size("grow") * planes) - 1.0


def is_even():
    return lax.rem(lax.axis_index("lat"), 2) == 0


def is_top():
    return lax.axis_index("grow") == lax.axis_size("grow") - 1


def load_planes(labels, seed, potential, lab, blend, mu, sems, first, count, at):
    zs, to = (pl.ds(first, count), pl.ds(at, count))
    copies = [
        pltpu.make_async_copy(seed.at[:, zs], blend.at[:, to], sems.at[0]),
        pltpu.make_async_copy(labels.at[zs], lab.at[to], sems.at[1]),
        pltpu.make_async_copy(potential.at[:, zs], mu.at[:, to], sems.at[2]),
    ]
    for copy in copies:
        copy.start()
    return copies


def initial_plane(kind, blend, mu, z):
    total = 1.0 + ((blend[0, z] + blend[1, z]) + (blend[2, z] + blend[3, z]))
    scale = 1.0 / total
    vals = [(jnp.where(kind[z] == a, 1.0, 0.0) + blend[a, z]) * scale for a in range(3)]
    return vals + [mu[0, z], mu[1, z]]


def first_kernel(labels, seed, potential, near, lab, blend, mu, sems):
    for copy in load_planes(labels, seed, potential, lab, blend, mu, sems, 0, early, 0):
        copy.wait()
    for z in range(early):
        for f, value in enumerate(initial_plane(lab, blend, mu, z)):
            near[z, f] = value


def start_kernel(labels, seed, potential, state, far, inner, outer):
    planes, height = labels.shape[0], labels.shape[1]
    for z in range(planes):
        vals = initial_plane(labels, seed, potential, z)
        for f in range(fields):
            state[z, f] = vals[f]
            if early <= z < shift + 2:
                at = ((z - early) * fields + f) * height
                far[at : at + height, :] = vals[f]

    def edges(after, before):
        for z in range(planes):
            for f in range(fields):
                at = 2 * (z * fields + f)
                before[at : at + 2, :] = state[z, f, 0:2, :]
                after[at : at + 2, :] = state[z, f, height - 2 : height, :]

    @pl.when(is_even())
    def _():
        edges(inner, outer)

    @pl.when(jnp.logical_not(is_even()))
    def _():
        edges(outer, inner)


def pack_kernel(far, inner, outer, near, done, inner_out, sem):
    at = far.shape[0] - edge_size
    slot = jnp.where(is_even(), 0, inner.shape[0])
    copy = pltpu.make_async_copy(outer.at[pl.ds(pl.multiple_of(slot, tile), edge_size)], done.at[at:], sem)
    copy.start()
    copy.wait()


def rows_kernel(near, late, inner):
    height = near.shape[2]

    def edges(row):
        for z in range(shift + 2):
            for f in range(fields):
                at = 2 * (z * fields + f)
                if z < early:
                    inner[at : at + 2, :] = near[z, f, row : row + 2, :]
                else:
                    first = ((z - early) * fields + f) * height + row
                    inner[at : at + 2, :] = late[first : first + 2, :]

    @pl.when(is_even())
    def _():
        edges(height - 2)

    @pl.when(jnp.logical_not(is_even()))
    def _():
        edges(0)


def gather_planes(dst, places, height):
    for i, (main, z, _, _) in enumerate(places):
        if len(main.shape) == 4:
            dst[i, :, 0:height, :] = main[z]
        else:
            for f in range(fields):
                dst[i, f, 0:height, :] = main[(z + f) * height : (z + f + 1) * height, :]

    def halo(inner_row, outer_row, slot):
        for i, (_, _, rows, (at_inner, at_outer)) in enumerate(places):
            at_outer = at_outer[slot]
            for f in range(fields):
                for row, at, ref in ((inner_row, at_inner, rows[0]), (outer_row, at_outer, rows[1])):
                    dst[i, f, height + row : height + row + 2, :] = ref[at + 2 * f : at + 2 * f + 2, :]

    @pl.when(is_even())
    def _():
        halo(0, 6, 0)

    @pl.when(jnp.logical_not(is_even()))
    def _():
        halo(6, 0, 1)


def own_places(state, inner, outer, zs):
    width = 2 * fields
    slots = (0, inner.shape[0])
    return [(state, z, (inner, outer), (width * z, [at + width * z for at in slots])) for z in zs]


def upper_places(near, late, inner, zs):
    width = 2 * fields
    outer = (shift + 2 - early) * fields * near.shape[2]
    return [
        (near if z < early else late, z if z < early else (z - early) * fields, (inner, late),
         (width * z, [outer + width * z] * 2))
        for z in zs
    ]


def steps(padded, half, done, planes, first, known, count, all_tiles):
    def one(i, _):
        step_plane(padded, i + 1, half, i + known, temp_of(i + first - 1 + known, planes), all_tiles, all_tiles)
        return 0

    def two(i, _):
        step_plane(half, i + 1, done, i, temp_of(i + first, planes), all_tiles - 1, all_tiles)
        return 0

    return (
        lambda: lax.fori_loop(0, count + 2 - known, one, 0),
        lambda: lax.fori_loop(0, count, two, 0),
    )


def own_kernel(state, inner, outer, done, carry, padded, half):
    planes, height = state.shape[0], state.shape[2]
    gather_planes(padded, own_places(state, inner, outer, range(shift - 2, planes)), height)
    count = planes - 2 - shift
    one, two = steps(padded, half, done, planes, shift, 0, count, height // tile + 1)
    one()
    two()
    carry[...] = half[count : count + 2]


def edge_kernel(state, inner, outer, near, late, upper_inner, carry, done, carry_out, padded, half):
    planes, height = state.shape[0], state.shape[2]
    gather_planes(
        padded,
        own_places(state, inner, outer, range(planes - 2, planes)) + upper_places(near, late, upper_inner, range(2)),
        height,
    )
    one, two = steps(padded, half, done, planes, planes - 2, 2, 2, height // tile + 1)
    half[0:2] = carry[...]

    @pl.when(is_top())
    def _():
        padded[2] = padded[1]

    one()

    @pl.when(is_top())
    def _():
        half[3] = half[2]

    two()
    carry_out[...] = half[2:4]


def write_planes(parts, phase, chem, extra, sems):
    copies = []
    for part, first in parts:
        count = part.shape[0]
        for f in range(fields):
            to = pl.ds(first, count)
            dst = phase.at[f, to] if f < 3 else chem.at[f - 3, to]
            copies.append(pltpu.make_async_copy(part.at[:, f], dst, sems.at[len(copies)]))
            copies[-1].start()
    for part, first in parts:
        for z in range(part.shape[0]):
            extra[first - parts[0][1] + z] = 1.0 - (part[z, 0] + part[z, 1] + part[z, 2])
    count = sum(part.shape[0] for part, _ in parts)
    copies.append(
        pltpu.make_async_copy(extra.at[0:count], phase.at[3, pl.ds(parts[0][1], count)], sems.at[len(copies)])
    )
    copies[-1].start()
    for copy in copies:
        copy.wait()


def write_liquid(inflow, table, phase, chem, liquid, sems):
    liquid[0] = jnp.ones(liquid.shape[1:], jnp.float32)
    liquid[1] = jnp.zeros(liquid.shape[1:], jnp.float32)

    def lookup(z, _):
        kind = inflow[z]
        for k in range(2):
            value = jnp.zeros(kind.shape, jnp.float32)
            for j in range(table.shape[0]):
                value = jnp.where(kind == j, table[j, k], value)
            liquid[2 + k, z] = value
        return 0

    lax.fori_loop(0, inflow.shape[0], lookup, 0)
    pairs = [(0, phase.at[0])] + [(1, phase.at[a]) for a in range(1, 4)]
    pairs += [(2 + k, chem.at[k]) for k in range(2)]
    copies = [pltpu.make_async_copy(liquid.at[j], dst, sems.at[i]) for i, (j, dst) in enumerate(pairs)]
    for copy in copies:
        copy.start()
    for copy in copies:
        copy.wait()


def upper_kernel(table, near, late, upper_inner, carry, middle, inflow, phase, chem, padded, half, low, liquid, sems):
    planes, height = phase.shape[1], near.shape[2]

    @pl.when(jnp.logical_not(is_top()))
    def _():
        gather_planes(padded, upper_places(near, late, upper_inner, range(shift + 2)), height)
        half[0:2] = carry[...]
        one, two = steps(padded, half, low, planes, planes, 2, shift, height // tile + 1)
        one()
        two()
        write_planes([(low, 0), (middle, shift)], phase, chem, liquid.at[0], sems)

    @pl.when(is_top())
    def _():
        write_liquid(inflow, table, phase, chem, liquid, sems)


def last_kernel(high, phase_in, chem_in, phase, chem, extra, sems):
    @pl.when(jnp.logical_not(is_top()))
    def _():
        write_planes([(high, phase.shape[1] - 2)], phase, chem, extra, sems)


def f32(*shape):
    return jax.ShapeDtypeStruct(shape, jnp.float32)


def down(block):
    return lax.ppermute(block, "grow", [(i, i - 1) for i in range(1, lax.axis_size("grow"))])


def call(kernel, out_shape, in_specs, scratch=(), out_specs=None, aliases={}, grant=10):
    return pl.pallas_call(
        kernel,
        out_shape=out_shape,
        in_specs=in_specs,
        out_specs=out_specs if out_specs is not None else jax.tree.map(lambda _: VMEM, out_shape),
        scratch_shapes=list(scratch),
        input_output_aliases=aliases,
        compiler_params=pltpu.CompilerParams(vmem_limit_bytes=grant * 1024 * 1024),
    )


def body(labels, seed_blend, potential, inflow_index, liquid_table):
    planes, height, width = labels.shape
    count = lax.axis_size("lat")
    padded_rows = height + tile

    def room(*shape):
        return pltpu.VMEM(shape, jnp.float32)

    near = call(
        first_kernel,
        f32(early, fields, height, width),
        [ANY] * 3,
        [
            pltpu.VMEM((early, height, width), jnp.int32),
            room(4, early, height, width),
            room(2, early, height, width),
            pltpu.SemaphoreType.DMA((3,)),
        ],
        grant=56,
    )(labels, seed_blend, potential)
    near = down(near)

    edge_rows = 2 * planes * fields
    state, far, inner, outer = call(
        start_kernel,
        (
            f32(planes, fields, height, width),
            f32((shift + 2 - early) * fields * height + edge_size, width),
            f32(edge_rows, width),
            f32(edge_rows, width),
        ),
        [VMEM] * 3,
    )(labels, seed_blend, potential)

    swap = [(i, i ^ 1) for i in range(count)]
    pairs = [[i, (i + 1) % count] for i in range(1, count, 2)]
    outer = lax.all_gather(outer, "lat", axis_index_groups=pairs, tiled=True)
    late, inner = call(
        pack_kernel,
        (jax.ShapeDtypeStruct(far.shape, far.dtype), jax.ShapeDtypeStruct(inner.shape, inner.dtype)),
        [ANY] * 4,
        [pltpu.SemaphoreType.DMA],
        (ANY, ANY),
        aliases={0: 0, 1: 1},
    )(far, inner, outer, near)
    late = down(late)
    inner = lax.ppermute(inner, "lat", swap)

    middle, carry = call(
        own_kernel,
        (f32(planes - 2 - shift, fields, height, width), f32(2, fields, padded_rows, width)),
        [VMEM] * 3,
        [room(planes - shift + 2, fields, padded_rows, width), room(planes - shift, fields, padded_rows, width)],
    )(state, inner, outer)
    middle = down(middle)

    upper_inner = call(rows_kernel, f32(edge_size, width), [VMEM] * 2)(near, late)
    upper_inner = lax.ppermute(upper_inner, "lat", swap)

    high, carry = call(
        edge_kernel,
        (f32(2, fields, height, width), f32(2, fields, padded_rows, width)),
        [VMEM] * 7,
        [room(4, fields, padded_rows, width), room(4, fields, padded_rows, width)],
    )(state, inner, outer, near, late, upper_inner, carry)
    high = down(high)

    outs = (f32(4, planes, height, width), f32(2, planes, height, width))
    phase, chem = call(
        upper_kernel,
        outs,
        [SMEM] + [VMEM] * 6,
        [
            room(shift + 2, fields, padded_rows, width),
            room(shift + 2, fields, padded_rows, width),
            room(shift, fields, height, width),
            room(4, planes, height, width),
            pltpu.SemaphoreType.DMA((2 * fields + 1,)),
        ],
        (ANY, ANY),
    )(liquid_table, near, late, upper_inner, carry, middle, inflow_index)
    return call(
        last_kernel,
        outs,
        [VMEM] + [ANY] * 2,
        [room(2, height, width), pltpu.SemaphoreType.DMA((fields + 1,))],
        (ANY, ANY),
        aliases={1: 0, 2: 1},
    )(high, phase, chem)


def solution(mesh):
    in_specs = (
        P("grow", "lat", None),
        P(None, "grow", "lat", None),
        P(None, "grow", "lat", None),
        P(None, "lat", None),
        P(),
    )
    out_specs = (P(None, "grow", "lat", None), P(None, "grow", "lat", None))
    return jax.shard_map(body, mesh=mesh, in_specs=in_specs, out_specs=out_specs, check_vma=False)
```

```python
import functools

import jax
import jax.numpy as jnp
from jax import lax
from jax.experimental import pallas as pl
from jax.experimental.pallas import tpu as pltpu
from jax.sharding import PartitionSpec as P

offset_table = ((0.0, 0.0), (0.6, -0.3), (-0.4, 0.5), (-0.2, -0.6))
latent_heat = (0.0, 0.8, 0.8, 0.8)
relax_rate = 0.1
diffusion = 0.05

shift = 2
early = 1
fields = 5
tile = 8
edge_size = -(-2 * fields * (shift + 2) // tile) * tile

VMEM = pl.BlockSpec(memory_space=pltpu.VMEM)
SMEM = pl.BlockSpec(memory_space=pltpu.SMEM)
ANY = pl.BlockSpec(memory_space=pl.ANY)


def step_tile(below, above, centre, before, after, temp):
    row = lax.broadcasted_iota(jnp.int32, centre[0].shape, 0)
    last = centre[0].shape[0] - 1
    width = centre[0].shape[1]
    laps = []
    for f in range(fields):
        c = centre[f]
        x_minus = pltpu.roll(jnp.where(row == last, before[f], c), 1, 0)
        x_plus = pltpu.roll(jnp.where(row == 0, after[f], c), last, 0)
        y_minus = pltpu.roll(c, 1, 1)
        y_plus = pltpu.roll(c, width - 1, 1)
        laps.append(
            (above[f] + below[f]) + (x_plus + x_minus) + (y_plus + y_minus) - 6.0 * c
        )
    p = list(centre[:3])
    p.append(1.0 - (p[0] + p[1] + p[2]))
    mu = centre[3:]
    common = 1.0 - (mu[0] * mu[0] + mu[1] * mu[1])
    react = []
    for a in range(4):
        e0, e1 = offset_table[a]
        w = common
        if a:
            w = w - (2.0 * e0) * mu[0] - (2.0 * e1) * mu[1]
            w = w + (2.0 * latent_heat[a] * temp - (e0 * e0 + e1 * e1))
        react.append(p[a] * (w + p[a] * (2.0 * p[a] - 3.0)))
    mean = 0.25 * ((react[0] + react[1]) + (react[2] + react[3]))
    new = [p[a] + relax_rate * (laps[a] + (mean - react[a])) for a in range(3)]
    new.append(1.0 - (new[0] + new[1] + new[2]))
    squares = [n * n for n in new]
    growth = [squares[a] - p[a] * p[a] for a in range(4)]
    sus = (squares[0] + squares[1]) + (squares[2] + squares[3])
    grown = (growth[0] + growth[1]) + (growth[2] + growth[3])
    mobile = diffusion * 0.1 + diffusion * squares[0]
    inverse = 1.0 / sus
    out = new[:3]
    for k in range(2):
        source = mu[k] * grown
        for a in range(1, 4):
            source = source + offset_table[a][k] * growth[a]
        out.append(mu[k] + (mobile * laps[3 + k] - source) * inverse)
    return out


def step_plane(src, at, dst, to, temp, tiles, all_tiles):
    for t in range(tiles):
        def rows(plane, u):
            u = (u + all_tiles) % all_tiles
            return [src[plane, f, u * tile : (u + 1) * tile, :] for f in range(fields)]

        new = step_tile(
            rows(at - 1, t), rows(at + 1, t), rows(at, t), rows(at, t - 1), rows(at, t + 1), temp
        )
        for f in range(fields):
            dst[to, f, t * tile : (t + 1) * tile, :] = new[f]


def temp_of(z, planes):
    plane = (lax.axis_index("grow") * planes + z).astype(jnp.float32)
    return 2.0 * (plane + 0.5) / float(lax.axis_size("grow") * planes) - 1.0


def is_even():
    return lax.rem(lax.axis_index("lat"), 2) == 0


def is_top():
    return lax.axis_index("grow") == lax.axis_size("grow") - 1


def load_planes(labels, seed, potential, lab, blend, mu, sems, first, count, at):
    zs, to = (pl.ds(first, count), pl.ds(at, count))
    copies = [
        pltpu.make_async_copy(seed.at[:, zs], blend.at[:, to], sems.at[0]),
        pltpu.make_async_copy(labels.at[zs], lab.at[to], sems.at[1]),
        pltpu.make_async_copy(potential.at[:, zs], mu.at[:, to], sems.at[2]),
    ]
    for copy in copies:
        copy.start()
    return copies


def initial_plane(kind, blend, mu, z):
    total = 1.0 + ((blend[0, z] + blend[1, z]) + (blend[2, z] + blend[3, z]))
    scale = 1.0 / total
    vals = [(jnp.where(kind[z] == a, 1.0, 0.0) + blend[a, z]) * scale for a in range(3)]
    return vals + [mu[0, z], mu[1, z]]


def first_kernel(labels, seed, potential, near, lab, blend, mu, sems):
    for copy in load_planes(labels, seed, potential, lab, blend, mu, sems, 0, early, 0):
        copy.wait()
    for z in range(early):
        for f, value in enumerate(initial_plane(lab, blend, mu, z)):
            near[z, f] = value


def start_kernel(labels, seed, potential, state, far, inner, outer):
    planes, height = labels.shape[0], labels.shape[1]
    for z in range(planes):
        vals = initial_plane(labels, seed, potential, z)
        for f in range(fields):
            state[z, f] = vals[f]
            if early <= z < shift + 2:
                at = ((z - early) * fields + f) * height
                far[at : at + height, :] = vals[f]

    def edges(after, before):
        for z in range(planes):
            for f in range(fields):
                at = 2 * (z * fields + f)
                before[at : at + 2, :] = state[z, f, 0:2, :]
                after[at : at + 2, :] = state[z, f, height - 2 : height, :]

    @pl.when(is_even())
    def _():
        edges(inner, outer)

    @pl.when(jnp.logical_not(is_even()))
    def _():
        edges(outer, inner)


def pack_kernel(far, inner, outer, near, done, inner_out):
    at = far.shape[0] - edge_size
    slot = pl.multiple_of(jnp.where(is_even(), 0, inner.shape[0]), tile)
    done[at:, :] = outer[pl.ds(slot, edge_size), :]


def rows_kernel(near, late, inner):
    height = near.shape[2]

    def edges(row):
        for z in range(shift + 2):
            for f in range(fields):
                at = 2 * (z * fields + f)
                if z < early:
                    inner[at : at + 2, :] = near[z, f, row : row + 2, :]
                else:
                    first = ((z - early) * fields + f) * height + row
                    inner[at : at + 2, :] = late[first : first + 2, :]

    @pl.when(is_even())
    def _():
        edges(height - 2)

    @pl.when(jnp.logical_not(is_even()))
    def _():
        edges(0)


def gather_planes(dst, places, height):
    for i, (main, z, _, _) in enumerate(places):
        if len(main.shape) == 4:
            dst[i, :, 0:height, :] = main[z]
        else:
            for f in range(fields):
                dst[i, f, 0:height, :] = main[(z + f) * height : (z + f + 1) * height, :]

    def halo(inner_row, outer_row, slot):
        for i, (_, _, rows, (at_inner, at_outer)) in enumerate(places):
            at_outer = at_outer[slot]
            for f in range(fields):
                for row, at, ref in ((inner_row, at_inner, rows[0]), (outer_row, at_outer, rows[1])):
                    dst[i, f, height + row : height + row + 2, :] = ref[at + 2 * f : at + 2 * f + 2, :]

    @pl.when(is_even())
    def _():
        halo(0, 6, 0)

    @pl.when(jnp.logical_not(is_even()))
    def _():
        halo(6, 0, 1)


def own_places(state, inner, outer, zs):
    width = 2 * fields
    slots = (0, inner.shape[0])
    return [(state, z, (inner, outer), (width * z, [at + width * z for at in slots])) for z in zs]


def upper_places(near, late, inner, zs):
    width = 2 * fields
    outer = (shift + 2 - early) * fields * near.shape[2]
    return [
        (near if z < early else late, z if z < early else (z - early) * fields, (inner, late),
         (width * z, [outer + width * z] * 2))
        for z in zs
    ]


def steps(padded, half, done, planes, first, known, count, all_tiles):
    def one(i, _):
        step_plane(padded, i + 1, half, i + known, temp_of(i + first - 1 + known, planes), all_tiles, all_tiles)
        return 0

    def two(i, _):
        step_plane(half, i + 1, done, i, temp_of(i + first, planes), all_tiles - 1, all_tiles)
        return 0

    return (
        lambda: lax.fori_loop(0, count + 2 - known, one, 0),
        lambda: lax.fori_loop(0, count, two, 0),
    )


def own_kernel(state, inner, outer, done, carry, padded, half):
    planes, height = state.shape[0], state.shape[2]
    gather_planes(padded, own_places(state, inner, outer, range(shift - 2, planes)), height)
    count = planes - 2 - shift
    one, two = steps(padded, half, done, planes, shift, 0, count, height // tile + 1)
    one()
    two()
    carry[...] = half[count : count + 2]


def edge_kernel(state, inner, outer, near, late, upper_inner, carry, done, carry_out, padded, half):
    planes, height = state.shape[0], state.shape[2]
    gather_planes(
        padded,
        own_places(state, inner, outer, range(planes - 2, planes)) + upper_places(near, late, upper_inner, range(2)),
        height,
    )
    one, two = steps(padded, half, done, planes, planes - 2, 2, 2, height // tile + 1)
    half[0:2] = carry[...]

    @pl.when(is_top())
    def _():
        padded[2] = padded[1]

    one()

    @pl.when(is_top())
    def _():
        half[3] = half[2]

    two()
    carry_out[...] = half[2:4]


def write_planes(parts, phase, chem, extra, sems):
    copies = []
    for part, first in parts:
        count = part.shape[0]
        for f in range(fields):
            to = pl.ds(first, count)
            dst = phase.at[f, to] if f < 3 else chem.at[f - 3, to]
            copies.append(pltpu.make_async_copy(part.at[:, f], dst, sems.at[len(copies)]))
            copies[-1].start()
    for part, first in parts:
        for z in range(part.shape[0]):
            extra[first - parts[0][1] + z] = 1.0 - (part[z, 0] + part[z, 1] + part[z, 2])
    count = sum(part.shape[0] for part, _ in parts)
    copies.append(
        pltpu.make_async_copy(extra.at[0:count], phase.at[3, pl.ds(parts[0][1], count)], sems.at[len(copies)])
    )
    copies[-1].start()
    for copy in copies:
        copy.wait()


def write_liquid(inflow, table, phase, chem, liquid, sems):
    liquid[0] = jnp.ones(liquid.shape[1:], jnp.float32)
    liquid[1] = jnp.zeros(liquid.shape[1:], jnp.float32)

    def lookup(z, _):
        kind = inflow[z]
        for k in range(2):
            value = jnp.zeros(kind.shape, jnp.float32)
            for j in range(table.shape[0]):
                value = jnp.where(kind == j, table[j, k], value)
            liquid[2 + k, z] = value
        return 0

    lax.fori_loop(0, inflow.shape[0], lookup, 0)
    pairs = [(0, phase.at[0])] + [(1, phase.at[a]) for a in range(1, 4)]
    pairs += [(2 + k, chem.at[k]) for k in range(2)]
    copies = [pltpu.make_async_copy(liquid.at[j], dst, sems.at[i]) for i, (j, dst) in enumerate(pairs)]
    for copy in copies:
        copy.start()
    for copy in copies:
        copy.wait()


def upper_kernel(table, near, late, upper_inner, carry, middle, inflow, phase, chem, padded, half, low, liquid, sems):
    planes, height = phase.shape[1], near.shape[2]

    @pl.when(jnp.logical_not(is_top()))
    def _():
        gather_planes(padded, upper_places(near, late, upper_inner, range(shift + 2)), height)
        half[0:2] = carry[...]
        one, two = steps(padded, half, low, planes, planes, 2, shift, height // tile + 1)
        one()
        two()
        write_planes([(low, 0), (middle, shift)], phase, chem, liquid.at[0], sems)

    @pl.when(is_top())
    def _():
        write_liquid(inflow, table, phase, chem, liquid, sems)


def last_kernel(high, phase_in, chem_in, phase, chem, extra, sems):
    @pl.when(jnp.logical_not(is_top()))
    def _():
        write_planes([(high, phase.shape[1] - 2)], phase, chem, extra, sems)


def f32(*shape):
    return jax.ShapeDtypeStruct(shape, jnp.float32)


def down(block):
    return lax.ppermute(block, "grow", [(i, i - 1) for i in range(1, lax.axis_size("grow"))])


def call(kernel, out_shape, in_specs, scratch=(), out_specs=None, aliases={}, grant=10):
    return pl.pallas_call(
        kernel,
        out_shape=out_shape,
        in_specs=in_specs,
        out_specs=out_specs if out_specs is not None else jax.tree.map(lambda _: VMEM, out_shape),
        scratch_shapes=list(scratch),
        input_output_aliases=aliases,
        compiler_params=pltpu.CompilerParams(vmem_limit_bytes=grant * 1024 * 1024),
    )


def body(labels, seed_blend, potential, inflow_index, liquid_table):
    planes, height, width = labels.shape
    count = lax.axis_size("lat")
    padded_rows = height + tile

    def room(*shape):
        return pltpu.VMEM(shape, jnp.float32)

    near = call(
        first_kernel,
        f32(early, fields, height, width),
        [ANY] * 3,
        [
            pltpu.VMEM((early, height, width), jnp.int32),
            room(4, early, height, width),
            room(2, early, height, width),
            pltpu.SemaphoreType.DMA((3,)),
        ],
        grant=56,
    )(labels, seed_blend, potential)
    near = down(near)

    edge_rows = 2 * planes * fields
    state, far, inner, outer = call(
        start_kernel,
        (
            f32(planes, fields, height, width),
            f32((shift + 2 - early) * fields * height + edge_size, width),
            f32(edge_rows, width),
            f32(edge_rows, width),
        ),
        [VMEM] * 3,
    )(labels, seed_blend, potential)

    swap = [(i, i ^ 1) for i in range(count)]
    pairs = [[i, (i + 1) % count] for i in range(1, count, 2)]
    outer = lax.all_gather(outer, "lat", axis_index_groups=pairs, tiled=True)
    late, inner = call(
        pack_kernel,
        (jax.ShapeDtypeStruct(far.shape, far.dtype), jax.ShapeDtypeStruct(inner.shape, inner.dtype)),
        [VMEM, ANY, VMEM, ANY],
        out_specs=(VMEM, ANY),
        aliases={0: 0, 1: 1},
    )(far, inner, outer, near)
    late = down(late)
    inner = lax.ppermute(inner, "lat", swap)

    middle, carry = call(
        own_kernel,
        (f32(planes - 2 - shift, fields, height, width), f32(2, fields, padded_rows, width)),
        [VMEM] * 3,
        [room(planes - shift + 2, fields, padded_rows, width), room(planes - shift, fields, padded_rows, width)],
    )(state, inner, outer)
    middle = down(middle)

    upper_inner = call(rows_kernel, f32(edge_size, width), [VMEM] * 2)(near, late)
    upper_inner = lax.ppermute(upper_inner, "lat", swap)

    high, carry = call(
        edge_kernel,
        (f32(2, fields, height, width), f32(2, fields, padded_rows, width)),
        [VMEM] * 7,
        [room(4, fields, padded_rows, width), room(4, fields, padded_rows, width)],
    )(state, inner, outer, near, late, upper_inner, carry)
    high = down(high)

    outs = (f32(4, planes, height, width), f32(2, planes, height, width))
    phase, chem = call(
        upper_kernel,
        outs,
        [SMEM] + [VMEM] * 6,
        [
            room(shift + 2, fields, padded_rows, width),
            room(shift + 2, fields, padded_rows, width),
            room(shift, fields, height, width),
            room(4, planes, height, width),
            pltpu.SemaphoreType.DMA((2 * fields + 1,)),
        ],
        (ANY, ANY),
    )(liquid_table, near, late, upper_inner, carry, middle, inflow_index)
    return call(
        last_kernel,
        outs,
        [VMEM] + [ANY] * 2,
        [room(2, height, width), pltpu.SemaphoreType.DMA((fields + 1,))],
        (ANY, ANY),
        aliases={1: 0, 2: 1},
    )(high, phase, chem)


def solution(mesh):
    in_specs = (
        P("grow", "lat", None),
        P(None, "grow", "lat", None),
        P(None, "grow", "lat", None),
        P(None, "lat", None),
        P(),
    )
    out_specs = (P(None, "grow", "lat", None), P(None, "grow", "lat", None))
    return jax.shard_map(body, mesh=mesh, in_specs=in_specs, out_specs=out_specs, check_vma=False)
```
